32 devices in a mesh: gx: 4 (over z), gy: 2 (over y), gz: 4 (over x, core).
Axes of the slice: x: 2, y: 2, z: 4, core: 2. Of those that a mesh axis runs over, the one named last changes fastest.
Arguments:
- ref_pos: float32 [256, 3, 128], P(('gx', 'gy', 'gz')), may hold values from -0.1 to 256, as said below
- displace: float32 [256, 3, 128], P(('gx', 'gy', 'gz')), may hold values from -0.1 to 0.1
- velocity: float32 [256, 3, 128], P(('gx', 'gy', 'gz')), may hold values from -15 to 15
- acceleration: float32 [256, 3, 128], P(('gx', 'gy', 'gz')), may hold values from -6 to 6
- new_owner: int32 [256], P(('gx', 'gy', 'gz')), may hold values from 0 to 31, as said below
- ghost_ids: int32 [768], P(('gx', 'gy', 'gz')), may hold values from 0 to 255, as said below
- pair_blocks: int32 [2, 6912], P(None, ('gx', 'gy', 'gz')), may hold values from 0 to 31, as said below
- pair_count: int32 [32], P(('gx', 'gy', 'gz')), may hold values from 1 to 216, as said below
- bond_bits: int32 [6912, 12, 128], P(('gx', 'gy', 'gz')), may hold values from 0 to 2047, as said below
Outputs:
- displace_new: float32 [256, 3, 128], P(('gx', 'gy', 'gz'))
- velocity_new: float32 [256, 3, 128], P(('gx', 'gy', 'gz'))
- acceleration_new: float32 [256, 3, 128], P(('gx', 'gy', 'gz'))
The draws below stay inside these ranges and needn't reach their ends.
Inputs may be any that keep to these rules, and one draw needn't show every extreme that they name: `new_owner`: each block's new owner is its own device or one of the 26 devices around it in the grid gx by gy by gz, wrapping around every axis; exactly 2 blocks of each device get another owner, and every device is the new owner of exactly 8 blocks. `ghost_ids`: block indices in the new layout; each names a block whose new owner is one of the 26 devices around the device of the list, wrapping around; a list may name a block more than once; a list names at most 3 entries whose blocks have the same owner, and exactly 3 for some owner in every list. `pair_blocks`: row 0 is a slot of the device (below 8); row 1 is an index into the device's 8 blocks followed by its 24 ghost blocks. `pair_count`: at least one device has all 216 slots live in every draw. `bond_bits`: bits of particles at 128 or beyond are not used. `ref_pos`: reference positions of two different particles are at least 0.65 apart.
All inputs are finite; a program needn't handle non-finite values. Where the reference program divides by a largest or mean magnitude, that divisor is 1e-20 or more.
Results may differ from the reference program's by a relative error of at most 0.0003.
Values sent between devices are 32-bit elements; how exact they have to be, the bound alone decides.
A program may use at most 64 MiB of HBM per device.

```python
import jax
import jax.numpy as jnp
import numpy as np
from jax import lax

BLOCK = 128
WORD_BITS = 11
BLK_DEV = 8
MOVE_MAX = 2
GHOSTS = 24
REQ_MAX = 3
PAIRS = 216
WORDS = 12
BLOCKS = 256
N_GX = 4
N_GY = 2
N_GZ = 4
DEVICES = 32


def step_table():
    values = np.array([-1, 0, 1], dtype=np.int32)
    offsets_all = np.stack(np.meshgrid(values, values, values, indexing='ij'), axis=-1).reshape(27, 3)
    return np.concatenate([offsets_all[:13], offsets_all[14:]], axis=0)


def grid_place(device):
    return (device // (N_GY * N_GZ), device // N_GZ % N_GY, device % N_GZ)


def neighbour_of(device, steps):
    place_x, place_y, place_z = grid_place(device)
    moved_x = (place_x + steps[..., 0]) % N_GX
    moved_y = (place_y + steps[..., 1]) % N_GY
    moved_z = (place_z + steps[..., 2]) % N_GZ
    return (moved_x * N_GY + moved_y) * N_GZ + moved_z


def crack_plane(key):
    return jax.random.randint(jax.random.fold_in(key, 99), (), 0, N_GX, dtype=jnp.int32)


def skew_step(key, coords, axis_number, leading):
    extents = (N_GX, N_GY, N_GZ)
    others = [number for number in range(3) if number != axis_number]
    table_shape = (extents[others[0]], extents[others[1]])
    if leading:
        lookup = 2 * jax.random.randint(key, table_shape, 0, 2, dtype=jnp.int32) - 1
    else:
        lookup = jax.random.randint(key, table_shape, -1, 2, dtype=jnp.int32)
    offset_step = lookup[coords[others[0]], coords[others[1]]]
    shifted_coords = list(coords)
    shifted_coords[axis_number] = (coords[axis_number] + offset_step) % extents[axis_number]
    return shifted_coords


def skew_target(key, leading_axis, places):
    candidates = []
    for start_axis in range(3):
        coords = list(places)
        for section_number in range(3):
            section_key = jax.random.fold_in(key, start_axis * 3 + section_number)
            coords = skew_step(section_key, coords, (start_axis + section_number) % 3, section_number == 0)
        candidates.append((coords[0] * N_GY + coords[1]) * N_GZ + coords[2])
    stacked = jnp.stack(candidates, axis=0)
    return stacked[leading_axis]


def draw_new_owner(key, part):
    slot_key, route_key, lead_key = jax.random.split(jax.random.fold_in(key, 11), 3)
    devices = jnp.arange(DEVICES, dtype=jnp.int32)
    places = grid_place(devices)
    leads = jax.random.randint(lead_key, (MOVE_MAX,), 0, 3, dtype=jnp.int32)
    target_list = [skew_target(jax.random.fold_in(route_key, mover_index), leads[mover_index], places) for mover_index in range(MOVE_MAX)]
    targets = jnp.stack(target_list, axis=1).astype(jnp.int32)
    slot_keys = jax.random.split(slot_key, DEVICES)
    leaving = jax.vmap(lambda single: jax.random.permutation(single, BLK_DEV)[:MOVE_MAX])(slot_keys)
    owners = jnp.broadcast_to(devices[:, None], (DEVICES, BLK_DEV))
    owners = owners.at[devices[:, None], leaving].set(targets)
    return owners.reshape(-1).astype(jnp.int32)


def draw_ghost_ids(key, part):
    order_key, slot_key, place_key = jax.random.split(jax.random.fold_in(key, 12), 3)
    steps_np = step_table()
    sizes_np = np.array([N_GX, N_GY, N_GZ], dtype=np.int32)
    barred = jnp.asarray(np.any((steps_np == -1) & (sizes_np[None, :] == 2), axis=1).astype(np.int32))
    step_rows = jnp.asarray(steps_np)
    devices = jnp.arange(DEVICES, dtype=jnp.int32)

    def choose(single):
        order = jax.random.permutation(single, 26).astype(jnp.int32)
        return order[jnp.argsort(barred[order], stable=True)]
    chosen = jax.vmap(choose)(jax.random.split(order_key, DEVICES))
    spread = jax.vmap(lambda single: jax.random.permutation(single, GHOSTS))(jax.random.split(place_key, DEVICES)).astype(jnp.int32)
    picked = jnp.take_along_axis(chosen, spread // REQ_MAX, axis=1)
    slot_ids = jax.random.randint(slot_key, (DEVICES, GHOSTS), 0, BLK_DEV, dtype=jnp.int32)
    owners = neighbour_of(devices[:, None], step_rows[picked])
    return (owners * BLK_DEV + slot_ids).reshape(-1).astype(jnp.int32)


def draw_pair_count(key, part):
    devices = jnp.arange(DEVICES, dtype=jnp.int32)
    modest = jax.random.randint(jax.random.fold_in(key, 13), (DEVICES,), PAIRS // 8 + 1, PAIRS // 3 + 1, dtype=jnp.int32)
    return jnp.where(devices // (N_GY * N_GZ) == crack_plane(key), PAIRS, modest).astype(jnp.int32)


def draw_pair_blocks(key, part):
    home_key, away_key = jax.random.split(jax.random.fold_in(key, 14))
    home_ids = jax.random.randint(home_key, (DEVICES * PAIRS,), 0, BLK_DEV, dtype=jnp.int32)
    away_ids = jax.random.randint(away_key, (DEVICES * PAIRS,), 0, BLK_DEV + GHOSTS, dtype=jnp.int32)
    return jnp.stack([home_ids, away_ids], axis=0)


def draw_bond_bits(key, part):
    full_shape = (DEVICES * PAIRS, WORDS, BLOCK)
    key_list = jax.random.split(jax.random.fold_in(key, 15), 7)
    ceiling = 2 ** WORD_BITS
    merged = jax.random.randint(key_list[0], full_shape, 0, ceiling, dtype=jnp.int32)
    for number in range(1, 5):
        merged = jnp.bitwise_and(merged, jax.random.randint(key_list[number], full_shape, 0, ceiling, dtype=jnp.int32))
    further = jnp.bitwise_and(jax.random.randint(key_list[5], full_shape, 0, ceiling, dtype=jnp.int32), jax.random.randint(key_list[6], full_shape, 0, ceiling, dtype=jnp.int32))
    device_x = jnp.arange(DEVICES * PAIRS, dtype=jnp.int32) // PAIRS // (N_GY * N_GZ)
    cracked = (device_x == crack_plane(key))[:, None, None]
    return jnp.where(cracked, jnp.bitwise_and(merged, further), merged).astype(jnp.int32)


def draw_ref_pos(key, part):
    lattice_key = jax.random.fold_in(jax.random.fold_in(key, 16), 0)
    index_b = jnp.arange(BLOCKS, dtype=jnp.int32)
    device = index_b // BLK_DEV
    inside = index_b % BLK_DEV
    place_x, place_y, place_z = grid_place(device)
    length_x = BLOCK // 16
    member = jnp.arange(BLOCK, dtype=jnp.int32)
    corner_x = (place_x * BLK_DEV + inside) * length_x
    coord_x = corner_x[:, None] + member[None, :] // 16
    coord_y = (place_y * 4)[:, None] + member[None, :] // 4 % 4
    coord_z = (place_z * 4)[:, None] + member[None, :] % 4
    lattice = jnp.stack([coord_x, coord_y, coord_z], axis=1).astype(jnp.float32)
    jitter = jax.random.uniform(lattice_key, (BLOCKS, 3, BLOCK), jnp.float32, -0.1, 0.1)
    return lattice + jitter


def draw_velocity(key, part):
    drawn_key = jax.random.fold_in(key, 17)
    full_shape = (BLOCKS, 3, BLOCK)
    drawn = jnp.clip(jax.random.normal(drawn_key, full_shape, jnp.float32), -5.0, 5.0)
    rising = 1.0 + 2.0 * jnp.arange(BLOCKS, dtype=jnp.float32) / (BLOCKS - 1)
    return drawn * rising[:, None, None]


def block_levels(stream_key, dims, cuts, low, top_value):
    factor_of, own = 1.0, jax.random.fold_in(stream_key, 6)
    for dim, blocks in cuts:
        steps = jnp.exp(jax.random.uniform(jax.random.fold_in(own, dim), (blocks,), jnp.float32, low / len(cuts), top_value / len(cuts)))
        factor_of = factor_of * jnp.repeat(steps, dims[dim] // blocks).reshape([-1 if axis == dim else 1 for axis in range(len(dims))])
    return factor_of


def gaussian(key, shape, scale, limit, cuts=(), kind=jnp.bfloat16):
    entries = scale * jax.random.normal(key, shape, jnp.float32)
    if cuts:
        entries = entries * block_levels(key, shape, cuts, -0.22, 0.18)
    return jnp.clip(entries, -limit, limit).astype(kind)


def setup_inputs(seed: int = 0) -> dict:
    seeds = jax.random.split(jax.random.key(seed), 10)
    ref_pos = draw_ref_pos(jax.random.fold_in(seeds[9], 71), 0)
    displace = jnp.clip(jax.random.uniform(seeds[1], (BLOCKS, 3, BLOCK), jnp.float32, -0.1, 0.1) * block_levels(seeds[1], (BLOCKS, 3, BLOCK), ((0, 32),), -0.4, 0.0), -0.1, 0.1)
    velocity = draw_velocity(jax.random.fold_in(seeds[9], 71), 0)
    acceleration = gaussian(seeds[3], (BLOCKS, 3, BLOCK), 1.0, 6.0, ((0, 32),), jnp.float32)
    new_owner = draw_new_owner(jax.random.fold_in(seeds[9], 71), 0)
    ghost_ids = draw_ghost_ids(jax.random.fold_in(seeds[9], 71), 0)
    pair_blocks = draw_pair_blocks(jax.random.fold_in(seeds[9], 71), 0)
    pair_count = draw_pair_count(jax.random.fold_in(seeds[9], 71), 0)
    bond_bits = draw_bond_bits(jax.random.fold_in(seeds[9], 71), 0)
    return {"ref_pos": ref_pos, "displace": displace, "velocity": velocity, "acceleration": acceleration, "new_owner": new_owner, "ghost_ids": ghost_ids, "pair_blocks": pair_blocks, "pair_count": pair_count, "bond_bits": bond_bits}


courant = 0.05
stiffness = 20.0

def tile_force(home_tile, away_tile, same_block, bit_words, live_mask):
    particles = home_tile.shape[2]
    ref_gap = away_tile[:, 0:3, :, None] - home_tile[:, 0:3, None, :]
    now_gap = ref_gap + (away_tile[:, 3:6, :, None] - home_tile[:, 3:6, None, :])
    rest_len = jnp.sqrt(lax.optimization_barrier(jnp.sum(ref_gap * ref_gap, axis=1)))
    now_len = jnp.sqrt(lax.optimization_barrier(jnp.sum(now_gap * now_gap, axis=1)))
    column = jnp.arange(particles).astype(jnp.int32)
    word_rows = jnp.take(bit_words, column // WORD_BITS, axis=1)
    intact = jnp.bitwise_and(jnp.right_shift(word_rows, (column % WORD_BITS)[None, :, None]), 1)
    selfish = same_block[:, None, None] & (column[:, None] == column[None, :])[None, :, :]
    weight = jnp.where(selfish, 0.0, intact.astype(jnp.float32)) * live_mask[:, None, None]
    safe_len = jnp.where(selfish, 1.0, rest_len)
    safe_now = jnp.where(selfish, 1.0, now_len)
    scaled = weight * ((now_len - rest_len) / safe_len) / safe_now
    return lax.optimization_barrier(jnp.sum(scaled[:, None, :, :] * now_gap, axis=2))

def reference(ref_pos, displace, velocity, acceleration, new_owner, ghost_ids, pair_blocks, pair_count, bond_bits):
    fastest = jnp.max(jnp.abs(velocity))
    timestep = courant / (fastest + 1e-06)
    halfway = velocity + 0.5 * timestep * acceleration
    shifted = displace + timestep * halfway
    ordering = jnp.argsort(new_owner, stable=True)
    ref_new = ref_pos[ordering]
    shifted_new = shifted[ordering]
    halfway_new = halfway[ordering]
    local_all = jnp.concatenate([ref_new, shifted_new], axis=1)
    particles = ref_pos.shape[2]
    locals_dev = local_all.reshape(DEVICES, BLK_DEV, 6, particles)
    ghosts_dev = local_all[ghost_ids].reshape(DEVICES, GHOSTS, 6, particles)
    homes = pair_blocks[0].reshape(DEVICES, PAIRS)
    aways = pair_blocks[1].reshape(DEVICES, PAIRS)
    bit_dev = bond_bits.reshape(DEVICES, PAIRS, WORDS, particles)

    def per_device(packed):
        local_set, ghost_set, home_ids, away_ids, bit_words, live_count = packed
        extended = jnp.concatenate([local_set, ghost_set], axis=0)
        live_mask = (jnp.arange(PAIRS).astype(jnp.int32) < live_count).astype(jnp.float32)
        tile_sum = tile_force(local_set[home_ids], extended[away_ids], home_ids == away_ids, bit_words, live_mask)
        return jnp.zeros((BLK_DEV, 3, particles), jnp.float32).at[home_ids].add(tile_sum)
    bond_sum = lax.map(per_device, (locals_dev, ghosts_dev, homes, aways, bit_dev, pair_count))
    acceleration_new = stiffness * bond_sum.reshape(BLOCKS, 3, particles)
    velocity_new = halfway_new + 0.5 * timestep * acceleration_new
    return (shifted_new, velocity_new, acceleration_new)
```

```python
import jax
import jax.numpy as jnp
from jax import lax
from jax.experimental import pallas as pl
from jax.experimental.pallas import tpu as pltpu
from jax.sharding import PartitionSpec as P

WORD_BITS = 11


courant = 0.05
stiffness = 20.0


def with_halo(shard, sides, width):
    for axis, dim in sides:
        size, length = (lax.axis_size(axis), shard.shape[dim])
        up = [(i, (i + 1) % size) for i in range(size)]
        down = [(j, i) for i, j in up]
        last = lax.slice_in_dim(shard, length - width, length, axis=dim)
        initial = lax.slice_in_dim(shard, 0, width, axis=dim)
        before = lax.ppermute(last, axis, up)
        after = lax.ppermute(initial, axis, down)
        shard = jnp.concatenate([before, shard, after], axis=dim)
    return shard


def grid_place(device, count_y, count_z):
    return (device // (count_y * count_z), device // count_z % count_y, device % count_z)


def around_index(offset, extent):
    wrapped = offset % extent
    return jnp.where(wrapped == 0, 1, jnp.where(wrapped == 1, 2, 0))


def neighbour_table(size_x, size_y, size_z, place_x, place_y, place_z):
    triple = jnp.arange(3, dtype=jnp.int32) - 1
    steps_x = (place_x + triple) % size_x
    steps_y = (place_y + triple) % size_y
    steps_z = (place_z + triple) % size_z
    devices = (steps_x[:, None, None] * size_y + steps_y[None, :, None]) * size_z + steps_z[
        None, None, :
    ]
    usable_x = jnp.array([size_x > 2, True, True])
    usable_y = jnp.array([size_y > 2, True, True])
    usable_z = jnp.array([size_z > 2, True, True])
    usable = usable_x[:, None, None] & usable_y[None, :, None] & usable_z[None, None, :]
    return (devices.reshape(27), usable.reshape(27))


def settle(states, owners, labels, usable, myself, blocks):
    chosen = usable & (owners == myself)
    before = chosen[None, :] & (labels[None, :] < labels[:, None])
    ranked = jnp.sum(before.astype(jnp.int32), axis=1)
    places = jnp.arange(blocks, dtype=jnp.int32)
    matches = chosen[None, :] & (ranked[None, :] == places[:, None])
    candidate_ids = jnp.arange(owners.shape[0], dtype=jnp.int32)
    chosen_ids = jnp.sum(jnp.where(matches, candidate_ids[None, :], 0), axis=1)
    return jnp.take(states, chosen_ids, axis=0)


def migrate(states, new_owner, myself, devices, usable, blocks):
    widths = states.shape[1:]
    order_ids = jnp.arange(blocks, dtype=jnp.int32)
    arrived, arrived_owner = (
        with_halo(states[None, None, None], (("gx", 0), ("gy", 1), ("gz", 2)), 1),
        with_halo(new_owner[None, None, None], (("gx", 0), ("gy", 1), ("gz", 2)), 1),
    )
    candidates = arrived.reshape((27 * blocks,) + widths)
    owners = arrived_owner.reshape(-1)
    labels = (devices[:, None] * blocks + order_ids[None, :]).reshape(-1)
    usable_all = jnp.repeat(usable, blocks)
    return settle(candidates, owners, labels, usable_all, myself, blocks)


def advance(displace, velocity, acceleration):
    fastest = lax.pmax(jnp.max(jnp.abs(velocity)), ("gx", "gy", "gz"))
    timestep = courant / (fastest + 1e-06)
    halfway = velocity + 0.5 * timestep * acceleration
    shifted = displace + timestep * halfway
    return (shifted, halfway, timestep)


SUBLANES = 8


def spread_away(ext_ref, turned_ref, wide_ref):
    extended, comps, particles = ext_ref.shape
    batch = turned_ref.shape[1] // comps
    aligned = SUBLANES * WORD_BITS

    def spread_batch(number, carry):
        rows = ext_ref[pl.ds(number * batch, batch)].reshape(batch * comps, particles)
        turned_ref[...] = rows.T
        for step in range(particles // SUBLANES):
            if step < WORD_BITS:
                column = turned_ref[pl.ds(step, SUBLANES, stride=WORD_BITS), :]
            else:
                start = aligned + (step - WORD_BITS) * SUBLANES
                column = turned_ref[pl.ds(start, SUBLANES), :]
            for block in range(batch):
                for comp in range(6):
                    place = block * comps + comp
                    wide_ref[number * batch + block, step, comp] = jnp.broadcast_to(
                        column[:, place : place + 1], (SUBLANES, particles)
                    )
        return carry

    lax.fori_loop(0, extended // batch, spread_batch, 0)


def tile_sum(home, away, words, wide_ref, particles):
    aligned = SUBLANES * WORD_BITS
    sublane = lax.broadcasted_iota(jnp.int32, (SUBLANES, particles), 0)
    sums = [jnp.zeros((SUBLANES, particles), jnp.float32) for _ in range(3)]
    front = words[0:SUBLANES]
    for step in range(particles // SUBLANES):
        if step < WORD_BITS:
            hit = jnp.bitwise_and(front, 1 << step)
        else:
            start = aligned + (step - WORD_BITS) * SUBLANES
            low, high = start // WORD_BITS, (start + SUBLANES - 1) // WORD_BITS
            row = jnp.broadcast_to(words[low : low + 1], (SUBLANES, particles))
            if high != low:
                upper = jnp.broadcast_to(words[high : high + 1], (SUBLANES, particles))
                row = jnp.where(sublane + start < high * WORD_BITS, row, upper)
            hit = jnp.bitwise_and(row, jnp.left_shift(1, (sublane + start) % WORD_BITS))
        other = [wide_ref[away, step, comp] for comp in range(6)]
        ref_gap = [other[k] - home[k] for k in range(3)]
        now_gap = [ref_gap[k] + (other[3 + k] - home[3 + k]) for k in range(3)]
        ref_sq = ref_gap[0] * ref_gap[0] + ref_gap[1] * ref_gap[1] + ref_gap[2] * ref_gap[2]
        now_sq = now_gap[0] * now_gap[0] + now_gap[1] * now_gap[1] + now_gap[2] * now_gap[2]
        scaled = jnp.where(hit != 0, lax.rsqrt(ref_sq) - lax.rsqrt(now_sq), 0.0)
        sums = [sums[k] + scaled * now_gap[k] for k in range(3)]
    return sums


def bond_kernel(
    pairs_ref, count_ref, step_ref, ext_ref, half_ref, bits_ref,
    velocity_ref, accel_ref, turned_ref, wide_ref, total_ref,
):
    blocks, _, particles = half_ref.shape
    words = bits_ref.shape[1]
    spread_away(ext_ref, turned_ref, wide_ref)
    total_ref[...] = jnp.zeros_like(total_ref)
    word_row = lax.broadcasted_iota(jnp.int32, (words, particles), 0)
    lane = lax.broadcasted_iota(jnp.int32, (words, particles), 1)
    own_bit = jnp.where(lane // WORD_BITS == word_row, jnp.left_shift(1, lane % WORD_BITS), 0)

    def add_pair(slot, carry):
        home_id = pairs_ref[0, slot]
        away_id = pairs_ref[1, slot]
        home = [
            jnp.broadcast_to(ext_ref[home_id, pl.ds(comp, 1), :], (SUBLANES, particles))
            for comp in range(6)
        ]
        same = jnp.where(home_id == away_id, 1, 0)
        bits = jnp.bitwise_and(bits_ref[slot], jnp.bitwise_not(own_bit * same))
        sums = tile_sum(home, away_id, bits, wide_ref, particles)
        for comp in range(3):
            total_ref[home_id, comp] += sums[comp]
        return carry

    lax.fori_loop(0, count_ref[0], add_pair, 0)
    accel = stiffness * jnp.sum(total_ref[...], axis=2)
    accel_ref[...] = accel
    velocity_ref[...] = half_ref[...] + 0.5 * step_ref[0] * accel


def bond_step(extended, halfway_new, timestep, pair_blocks, pair_count, bond_bits):
    ext_blocks, comps, particles = extended.shape
    blocks = halfway_new.shape[0]
    batch = 4 if ext_blocks % 4 == 0 else 1
    shape = jax.ShapeDtypeStruct(halfway_new.shape, jnp.float32)
    smem = pl.BlockSpec(memory_space=pltpu.SMEM)
    vmem = pl.BlockSpec(memory_space=pltpu.VMEM)
    return pl.pallas_call(
        bond_kernel,
        out_shape=(shape, shape),
        in_specs=[smem, smem, smem, vmem, vmem, vmem],
        out_specs=(vmem, vmem),
        scratch_shapes=[
            pltpu.VMEM((particles, batch * comps), jnp.float32),
            pltpu.VMEM((ext_blocks, particles // SUBLANES, 6, SUBLANES, particles), jnp.float32),
            pltpu.VMEM((blocks, 3, SUBLANES, particles), jnp.float32),
        ],
        compiler_params=pltpu.CompilerParams(vmem_limit_bytes=40 * 1024 * 1024),
    )(pair_blocks, pair_count, timestep.reshape(1), extended, halfway_new, bond_bits)


def per_device(
    ref_pos,
    displace,
    velocity,
    acceleration,
    new_owner,
    ghost_ids,
    pair_blocks,
    pair_count,
    bond_bits,
):
    blocks = ref_pos.shape[0]
    particles = ref_pos.shape[2]
    size_x = lax.axis_size("gx")
    size_y = lax.axis_size("gy")
    size_z = lax.axis_size("gz")
    place_x = lax.axis_index("gx")
    place_y = lax.axis_index("gy")
    place_z = lax.axis_index("gz")
    myself = (place_x * size_y + place_y) * size_z + place_z
    devices, usable = neighbour_table(size_x, size_y, size_z, place_x, place_y, place_z)
    settled = migrate(
        jnp.concatenate([ref_pos, displace, velocity, acceleration], axis=1),
        new_owner,
        myself,
        devices,
        usable,
        blocks,
    )
    ref_new = settled[:, 0:3]
    shifted_new, halfway_new, timestep = advance(settled[:, 3:6], settled[:, 6:9], settled[:, 9:12])
    local_set = jnp.concatenate([ref_new, shifted_new], axis=1)
    ghost_dev = ghost_ids // blocks
    ghost_slot = ghost_ids % blocks
    ghost_x, ghost_y, ghost_z = grid_place(ghost_dev, size_y, size_z)
    ghost_cell = (
        around_index(ghost_x - place_x, size_x) * 9
        + around_index(ghost_y - place_y, size_y) * 3
        + around_index(ghost_z - place_z, size_z)
    )
    beside_all = with_halo(local_set[None, None, None], (("gx", 0), ("gy", 1), ("gz", 2)), 1)
    beside_all = beside_all.reshape(27 * blocks, 6, particles)
    ghost_set = jnp.take(beside_all, ghost_cell * blocks + ghost_slot, axis=0)
    extended = jnp.concatenate([local_set, ghost_set], axis=0)
    extended = jnp.pad(extended, ((0, 0), (0, 2), (0, 0)))
    velocity_new, acceleration_new = bond_step(
        extended, halfway_new, timestep, pair_blocks, pair_count, bond_bits
    )
    return (shifted_new, velocity_new, acceleration_new)


def solution(mesh):
    in_specs = (
        P(("gx", "gy", "gz"), None, None),
        P(("gx", "gy", "gz"), None, None),
        P(("gx", "gy", "gz"), None, None),
        P(("gx", "gy", "gz"), None, None),
        P(("gx", "gy", "gz")),
        P(("gx", "gy", "gz")),
        P(None, ("gx", "gy", "gz")),
        P(("gx", "gy", "gz")),
        P(("gx", "gy", "gz"), None, None),
    )
    out_specs = (
        P(("gx", "gy", "gz"), None, None),
        P(("gx", "gy", "gz"), None, None),
        P(("gx", "gy", "gz"), None, None),
    )
    return jax.shard_map(
        per_device, mesh=mesh, in_specs=in_specs, out_specs=out_specs, check_vma=False
    )
```

```python
import functools

import jax
import jax.numpy as jnp
from jax import lax
from jax.experimental import pallas as pl
from jax.experimental.pallas import tpu as pltpu
from jax.sharding import PartitionSpec as P

WORD_BITS = 11


courant = 0.05
stiffness = 20.0


MESH = pl.DeviceIdType.MESH
AXES = ("gx", "gy", "gz")
MOVERS = 2
STATE = 12
OWNER_ROW = MOVERS * STATE


def reach(size):
    return (0,) if size == 1 else (0, 1) if size == 2 else (-1, 0, 1)


def cell_rank(place, step, size):
    if size < 3:
        return (place + step) % size
    first = (size - place) // size
    last = (place + 1) // size
    return (step + 1 + 2 * first + last) % 3


def cell_of(places, steps, sizes):
    cell = 0
    for place, step, size in zip(places, steps, sizes):
        cell = cell * len(reach(size)) + cell_rank(place, step, size)
    return cell


def neighbour_steps(sizes):
    every = [(x, y, z) for x in reach(sizes[0]) for y in reach(sizes[1]) for z in reach(sizes[2])]
    return [steps for steps in every if steps != (0, 0, 0)]


def exchange_kernel(
    sizes,
    owner_ref, ref_ref, disp_ref, vel_ref, acc_ref,
    around_ref, half_ref, step_ref,
    arrived_ref, peak_ref, send_sems, recv_sems,
):
    blocks, dims, particles = ref_ref.shape
    total = sizes[0] * sizes[1] * sizes[2]
    steps_all = neighbour_steps(sizes)
    cells = len(steps_all) + 1
    places = [lax.axis_index(name) for name in AXES]
    myself = (places[0] * sizes[1] + places[1]) * sizes[2] + places[2]
    mine = cell_of(places, (0, 0, 0), sizes)

    def coords(device):
        return (device // (sizes[1] * sizes[2]), device // sizes[2] % sizes[1], device % sizes[2])

    def greet(number, carry):
        pl.semaphore_signal(
            barrier, inc=1, device_id=coords((myself + number) % total), device_id_type=MESH
        )
        return carry

    barrier = pltpu.get_barrier_semaphore()
    lax.fori_loop(1, total, greet, 0)

    speeds = jnp.max(jnp.abs(vel_ref[...]), axis=0)
    peak_ref[myself] = jnp.max(speeds, axis=0, keepdims=True)
    leavers = [jnp.int32(0) for _ in range(MOVERS)]
    seen = jnp.int32(0)
    for block in range(blocks):
        leaves = jnp.where(owner_ref[block] != myself, 1, 0)
        for order in range(MOVERS):
            leavers[order] += block * leaves * jnp.where(seen == order, 1, 0)
        seen += leaves
    for order in range(MOVERS):
        for part, source in enumerate((ref_ref, disp_ref, vel_ref, acc_ref)):
            arrived_ref[mine, pl.ds(order * STATE + part * dims, dims), :] = source[leavers[order]]
        owner = jnp.full((1, particles), owner_ref[leavers[order]], jnp.int32)
        arrived_ref[mine, pl.ds(OWNER_ROW + order, 1), :] = owner.astype(jnp.float32)
    rest = arrived_ref.shape[1] - OWNER_ROW - MOVERS
    arrived_ref[mine, pl.ds(OWNER_ROW + MOVERS, rest), :] = jnp.zeros((rest, particles), jnp.float32)

    pl.semaphore_wait(barrier, total - 1)

    def peak_copy(number):
        return pltpu.make_async_remote_copy(
            src_ref=peak_ref.at[myself],
            dst_ref=peak_ref.at[myself],
            send_sem=send_sems.at[0],
            recv_sem=recv_sems.at[0],
            device_id=coords((myself + number) % total),
            device_id_type=MESH,
        )

    def send_peak(number, carry):
        peak_copy(number).start()
        return carry

    def halo_copy(ref, steps, kind):
        target = [(place + step) % size for place, step, size in zip(places, steps, sizes)]
        back = [-step for step in steps]
        return pltpu.make_async_remote_copy(
            src_ref=ref.at[mine],
            dst_ref=ref.at[cell_of(target, back, sizes)],
            send_sem=send_sems.at[kind],
            recv_sem=recv_sems.at[kind],
            device_id=tuple(target),
            device_id_type=MESH,
        )

    def all_bytes(ref, kind):
        part = ref.at[pl.ds(0, ref.shape[0] - 1)]
        return pltpu.make_async_copy(part, part, recv_sems.at[kind]), pltpu.make_async_copy(
            part, part, send_sems.at[kind]
        )

    lax.fori_loop(1, total, send_peak, 0)
    for steps in steps_all:
        halo_copy(arrived_ref, steps, 1).start()
    peak_in, peak_out = all_bytes(peak_ref, 0)
    state_in, state_out = all_bytes(arrived_ref, 1)
    around_in, around_out = all_bytes(around_ref, 2)
    peak_in.wait()
    fastest = jnp.max(jnp.max(peak_ref[...], axis=0), axis=1, keepdims=True)
    timestep = jnp.broadcast_to(courant / (fastest + 1e-06), (blocks, particles))
    step_ref[...] = timestep

    state_in.wait()
    slot = lax.broadcasted_iota(jnp.int32, (blocks, particles), 0).astype(jnp.float32)
    settled = [jnp.zeros((blocks, particles), jnp.float32) for _ in range(STATE)]
    count = jnp.zeros((1, particles), jnp.float32)
    own_start = jnp.zeros((1, particles), jnp.float32)
    name = myself.astype(jnp.float32)
    for cell in range(cells):
        own = jnp.where(mine == cell, 1.0, 0.0)
        own_start = own_start + own * count
        count = count + own * (blocks - MOVERS)
        for order in range(MOVERS):
            owner = arrived_ref[cell, pl.ds(OWNER_ROW + order, 1), :]
            hit = owner == name
            chosen = slot == jnp.where(hit, count, -1.0)
            for comp in range(STATE):
                row = arrived_ref[cell, pl.ds(order * STATE + comp, 1), :]
                settled[comp] = jnp.where(chosen, row, settled[comp])
            count = count + jnp.where(hit, 1.0, 0.0)
    stayed = jnp.int32(0)
    for block in range(blocks):
        stays = jnp.where(owner_ref[block] == myself, 1, 0)
        offset = jnp.where(stays == 1, stayed, -2 * blocks * MOVERS * cells).astype(jnp.float32)
        chosen = slot == own_start + offset
        for part, source in enumerate((ref_ref, disp_ref, vel_ref, acc_ref)):
            for dim in range(dims):
                comp = part * dims + dim
                row = source[block, pl.ds(dim, 1), :]
                settled[comp] = jnp.where(chosen, row, settled[comp])
        stayed += stays

    for dim in range(dims):
        halfway = settled[2 * dims + dim] + 0.5 * timestep * settled[3 * dims + dim]
        half_ref[dim] = halfway
        around_ref[mine, dim] = settled[dim]
        around_ref[mine, dims + dim] = settled[dims + dim] + timestep * halfway

    for steps in steps_all:
        halo_copy(around_ref, steps, 2).start()
    around_in.wait()
    peak_out.wait()
    state_out.wait()
    around_out.wait()


def exchange(sizes, new_owner, ref_pos, displace, velocity, acceleration):
    blocks, dims, particles = ref_pos.shape
    cells = len(neighbour_steps(sizes)) + 1
    total = sizes[0] * sizes[1] * sizes[2]
    rows = -(-(OWNER_ROW + MOVERS) // SUBLANES) * SUBLANES
    smem = pl.BlockSpec(memory_space=pltpu.SMEM)
    vmem = pl.BlockSpec(memory_space=pltpu.VMEM)
    return pl.pallas_call(
        functools.partial(exchange_kernel, sizes),
        out_shape=(
            jax.ShapeDtypeStruct((cells, 2 * dims, blocks, particles), jnp.float32),
            jax.ShapeDtypeStruct((dims, blocks, particles), jnp.float32),
            jax.ShapeDtypeStruct((blocks, particles), jnp.float32),
        ),
        in_specs=[smem, vmem, vmem, vmem, vmem],
        out_specs=(vmem, vmem, vmem),
        scratch_shapes=[
            pltpu.VMEM((cells, rows, particles), jnp.float32),
            pltpu.VMEM((total, 1, particles), jnp.float32),
            pltpu.SemaphoreType.DMA((3,)),
            pltpu.SemaphoreType.DMA((3,)),
        ],
        compiler_params=pltpu.CompilerParams(
            collective_id=0, has_side_effects=True, vmem_limit_bytes=16 * 1024 * 1024
        ),
    )(new_owner, ref_pos, displace, velocity, acceleration)


SUBLANES = 8


def spread_away(index_ref, around_ref, rows_ref, turned_ref, wide_ref):
    extended, comps, particles = rows_ref.shape
    blocks = around_ref.shape[2]
    batch = turned_ref.shape[1] // comps
    aligned = SUBLANES * WORD_BITS

    def spread_batch(number, carry):
        for block in range(batch):
            index = index_ref[number * batch + block]
            for comp in range(6):
                rows_ref[number * batch + block, pl.ds(comp, 1), :] = around_ref[
                    index // blocks, comp, pl.ds(index % blocks, 1), :
                ]
        rows = rows_ref[pl.ds(number * batch, batch)].reshape(batch * comps, particles)
        turned_ref[...] = rows.T
        for step in range(particles // SUBLANES):
            if step < WORD_BITS:
                column = turned_ref[pl.ds(step, SUBLANES, stride=WORD_BITS), :]
            else:
                start = aligned + (step - WORD_BITS) * SUBLANES
                column = turned_ref[pl.ds(start, SUBLANES), :]
            for block in range(batch):
                for comp in range(6):
                    place = block * comps + comp
                    wide_ref[number * batch + block, step, comp] = jnp.broadcast_to(
                        column[:, place : place + 1], (SUBLANES, particles)
                    )
        return carry

    lax.fori_loop(0, extended // batch, spread_batch, 0)


def tile_sum(home, away, words, wide_ref, particles):
    aligned = SUBLANES * WORD_BITS
    sublane = lax.broadcasted_iota(jnp.int32, (SUBLANES, particles), 0)
    sums = [jnp.zeros((SUBLANES, particles), jnp.float32) for _ in range(3)]
    front = words[0:SUBLANES]
    for step in range(particles // SUBLANES):
        if step < WORD_BITS:
            hit = jnp.bitwise_and(front, 1 << step)
        else:
            start = aligned + (step - WORD_BITS) * SUBLANES
            low, high = start // WORD_BITS, (start + SUBLANES - 1) // WORD_BITS
            row = jnp.broadcast_to(words[low : low + 1], (SUBLANES, particles))
            if high != low:
                upper = jnp.broadcast_to(words[high : high + 1], (SUBLANES, particles))
                row = jnp.where(sublane + start < high * WORD_BITS, row, upper)
            hit = jnp.bitwise_and(row, jnp.left_shift(1, (sublane + start) % WORD_BITS))
        other = [wide_ref[away, step, comp] for comp in range(6)]
        ref_gap = [other[k] - home[k] for k in range(3)]
        now_gap = [ref_gap[k] + (other[3 + k] - home[3 + k]) for k in range(3)]
        ref_sq = ref_gap[0] * ref_gap[0] + ref_gap[1] * ref_gap[1] + ref_gap[2] * ref_gap[2]
        now_sq = now_gap[0] * now_gap[0] + now_gap[1] * now_gap[1] + now_gap[2] * now_gap[2]
        scaled = jnp.where(hit != 0, lax.rsqrt(ref_sq) - lax.rsqrt(now_sq), 0.0)
        sums = [sums[k] + scaled * now_gap[k] for k in range(3)]
    return sums


def bond_kernel(
    pairs_ref, count_ref, index_ref, around_ref, half_ref, step_ref, bits_ref,
    displace_ref, velocity_ref, accel_ref, rows_ref, turned_ref, wide_ref, total_ref,
):
    blocks, _, particles = accel_ref.shape
    words = bits_ref.shape[1]
    rows_ref[...] = jnp.zeros_like(rows_ref)
    spread_away(index_ref, around_ref, rows_ref, turned_ref, wide_ref)
    total_ref[...] = jnp.zeros_like(total_ref)
    word_row = lax.broadcasted_iota(jnp.int32, (words, particles), 0)
    lane = lax.broadcasted_iota(jnp.int32, (words, particles), 1)
    own_bit = jnp.where(lane // WORD_BITS == word_row, jnp.left_shift(1, lane % WORD_BITS), 0)

    def add_pair(slot, carry):
        home_id = pairs_ref[0, slot]
        away_id = pairs_ref[1, slot]
        home = [
            jnp.broadcast_to(rows_ref[home_id, pl.ds(comp, 1), :], (SUBLANES, particles))
            for comp in range(6)
        ]
        same = jnp.where(home_id == away_id, 1, 0)
        bits = jnp.bitwise_and(bits_ref[slot], jnp.bitwise_not(own_bit * same))
        sums = tile_sum(home, away_id, bits, wide_ref, particles)
        for comp in range(3):
            total_ref[home_id, comp] += sums[comp]
        return carry

    lax.fori_loop(0, count_ref[0], add_pair, 0)
    accel = stiffness * jnp.sum(total_ref[...], axis=2)
    accel_ref[...] = accel
    mine = index_ref[0] // blocks
    for comp in range(3):
        displace_ref[:, comp, :] = around_ref[mine, 3 + comp]
        velocity_ref[:, comp, :] = half_ref[comp] + 0.5 * step_ref[...] * accel[:, comp, :]


def bond_step(index, around, half, step, pair_blocks, pair_count, bond_bits):
    blocks, particles = step.shape
    extended = index.shape[0]
    batch = 4 if extended % 4 == 0 else 1
    shape = jax.ShapeDtypeStruct((blocks, 3, particles), jnp.float32)
    smem = pl.BlockSpec(memory_space=pltpu.SMEM)
    vmem = pl.BlockSpec(memory_space=pltpu.VMEM)
    return pl.pallas_call(
        bond_kernel,
        out_shape=(shape, shape, shape),
        in_specs=[smem, smem, smem, vmem, vmem, vmem, vmem],
        out_specs=(vmem, vmem, vmem),
        scratch_shapes=[
            pltpu.VMEM((extended, SUBLANES, particles), jnp.float32),
            pltpu.VMEM((particles, batch * SUBLANES), jnp.float32),
            pltpu.VMEM((extended, particles // SUBLANES, 6, SUBLANES, particles), jnp.float32),
            pltpu.VMEM((blocks, 3, SUBLANES, particles), jnp.float32),
        ],
        compiler_params=pltpu.CompilerParams(vmem_limit_bytes=40 * 1024 * 1024),
    )(pair_blocks, pair_count, index, around, half, step, bond_bits)


def per_device(
    ref_pos,
    displace,
    velocity,
    acceleration,
    new_owner,
    ghost_ids,
    pair_blocks,
    pair_count,
    bond_bits,
):
    blocks = ref_pos.shape[0]
    sizes = tuple(lax.axis_size(name) for name in AXES)
    places = [lax.axis_index(name) for name in AXES]
    around, half, step = exchange(sizes, new_owner, ref_pos, displace, velocity, acceleration)
    ghost_dev = ghost_ids // blocks
    ghost_places = (
        ghost_dev // (sizes[1] * sizes[2]),
        ghost_dev // sizes[2] % sizes[1],
        ghost_dev % sizes[2],
    )
    moves = []
    for ghost, place, size in zip(ghost_places, places, sizes):
        apart = (ghost - place) % size
        moves.append(jnp.where(apart == size - 1, -1, apart) if size > 2 else apart)
    ghost_cell = cell_of(places, moves, sizes)
    own_cell = cell_of(places, (0, 0, 0), sizes)
    index = jnp.concatenate([
        own_cell * blocks + jnp.arange(blocks, dtype=jnp.int32),
        ghost_cell * blocks + ghost_ids % blocks,
    ])
    return bond_step(index, around, half, step, pair_blocks, pair_count, bond_bits)


def solution(mesh):
    in_specs = (
        P(("gx", "gy", "gz"), None, None),
        P(("gx", "gy", "gz"), None, None),
        P(("gx", "gy", "gz"), None, None),
        P(("gx", "gy", "gz"), None, None),
        P(("gx", "gy", "gz")),
        P(("gx", "gy", "gz")),
        P(None, ("gx", "gy", "gz")),
        P(("gx", "gy", "gz")),
        P(("gx", "gy", "gz"), None, None),
    )
    out_specs = (
        P(("gx", "gy", "gz"), None, None),
        P(("gx", "gy", "gz"), None, None),
        P(("gx", "gy", "gz"), None, None),
    )
    return jax.shard_map(
        per_device, mesh=mesh, in_specs=in_specs, out_specs=out_specs, check_vma=False
    )
```

```python
import functools

import jax
import jax.numpy as jnp
from jax import lax
from jax.experimental import pallas as pl
from jax.experimental.pallas import tpu as pltpu
from jax.sharding import PartitionSpec as P

WORD_BITS = 11


courant = 0.05
stiffness = 20.0


MESH = pl.DeviceIdType.MESH
AXES = ("gx", "gy", "gz")
MOVERS = 2
REQUESTS = 3
STATE = 12
SUBLANES = 8
OWNER_ROW = 1
GHOST_ROW = OWNER_ROW + MOVERS
CARD = GHOST_ROW + 1
UNROLLED = 64
TOGETHER = 2


def reach(size):
    return (0,) if size == 1 else (0, 1) if size == 2 else (-1, 0, 1)


def cell_rank(place, step, size):
    if size < 3:
        return (place + step) % size
    first = (size - place) // size
    last = (place + 1) // size
    return (step + 1 + 2 * first + last) % 3


def cell_of(places, steps, sizes):
    cell = 0
    for place, step, size in zip(places, steps, sizes):
        cell = cell * len(reach(size)) + cell_rank(place, step, size)
    return cell


def neighbour_steps(sizes):
    every = [(x, y, z) for x in reach(sizes[0]) for y in reach(sizes[1]) for z in reach(sizes[2])]
    return [steps for steps in every if steps != (0, 0, 0)]


def cell_target(places, ranks, sizes):
    target = []
    for place, rank, size in zip(places, ranks, sizes):
        if size < 3:
            target.append(jnp.int32(rank))
        else:
            first = (size - place) // size
            last = (place + 1) // size
            target.append((place + (rank + 6 - 2 * first - last) % 3 - 1 + size) % size)
    return target


def exchange_kernel(
    sizes,
    owner_ref, ghost_ref, ref_ref, disp_ref, vel_ref, acc_ref,
    local_ref, ghosts_ref, half_ref, step_ref,
    arrived_ref, card_ref, pack_ref, list_ref, ask_ref, flat_ref,
    send_sems, recv_sems,
):
    dims, blocks, particles = ref_ref.shape
    total = sizes[0] * sizes[1] * sizes[2]
    steps_all = neighbour_steps(sizes)
    cells = len(steps_all) + 1
    extents = [len(reach(size)) for size in sizes]
    ranks_all = [
        (x, y, z) for x in range(extents[0]) for y in range(extents[1]) for z in range(extents[2])
    ]
    places = [lax.axis_index(name) for name in AXES]
    myself = (places[0] * sizes[1] + places[1]) * sizes[2] + places[2]
    mine = cell_of(places, (0, 0, 0), sizes)
    sources = (ref_ref, disp_ref, vel_ref, acc_ref)

    def to_others(action):
        if total <= UNROLLED:
            coords = [
                [(place + step) % size for step in range(size)]
                for place, size in zip(places, sizes)
            ]
            for x in range(sizes[0]):
                for y in range(sizes[1]):
                    for z in range(sizes[2]):
                        if (x, y, z) != (0, 0, 0):
                            action((coords[0][x], coords[1][y], coords[2][z]))
        else:

            def act(number, carry):
                device = (myself + number) % total
                rest = device // sizes[2]
                action((rest // sizes[1], rest % sizes[1], device % sizes[2]))
                return carry

            lax.fori_loop(1, total, act, 0)

    barrier = pltpu.get_barrier_semaphore()
    to_others(
        lambda target: pl.semaphore_signal(barrier, inc=1, device_id=target, device_id_type=MESH)
    )

    leavers = [jnp.int32(0) for _ in range(MOVERS)]
    seen = jnp.int32(0)
    for block in range(blocks):
        leaves = jnp.where(owner_ref[block] != myself, 1, 0)
        for order in range(MOVERS):
            leavers[order] += block * leaves * jnp.where(seen == order, 1, 0)
        seen += leaves
    speeds = jnp.max(jnp.abs(vel_ref[...]), axis=0)
    card_ref[myself, pl.ds(0, 1), :] = jnp.max(speeds, axis=0, keepdims=True)
    for order in range(MOVERS):
        owner = jnp.full((1, particles), owner_ref[leavers[order]], jnp.int32)
        card_ref[myself, pl.ds(OWNER_ROW + order, 1), :] = owner.astype(jnp.float32)
    card_ref[myself, pl.ds(GHOST_ROW, 1), :] = ghost_ref[...]
    for order in range(MOVERS):
        for part, source in enumerate(sources):
            for dim in range(dims):
                row = order * STATE + part * dims + dim
                arrived_ref[mine, pl.ds(row, 1), :] = source[dim, pl.ds(leavers[order], 1), :]

    pl.semaphore_wait(barrier, total - 1)

    def send_card(target):
        pltpu.make_async_remote_copy(
            src_ref=card_ref.at[myself],
            dst_ref=card_ref.at[myself],
            send_sem=send_sems.at[0],
            recv_sem=recv_sems.at[0],
            device_id=target,
            device_id_type=MESH,
        ).start()

    def send_halo(steps, source_of, ref, kind):
        target = [(place + step) % size for place, step, size in zip(places, steps, sizes)]
        back = [-step for step in steps]
        pltpu.make_async_remote_copy(
            src_ref=source_of(cell_of(places, steps, sizes)),
            dst_ref=ref.at[cell_of(target, back, sizes)],
            send_sem=send_sems.at[kind],
            recv_sem=recv_sems.at[kind],
            device_id=tuple(target),
            device_id_type=MESH,
        ).start()

    def all_bytes(ref, sem):
        part = ref.at[pl.ds(0, ref.shape[0] - 1)]
        return pltpu.make_async_copy(part, part, sem)

    to_others(send_card)
    for steps in steps_all:
        send_halo(steps, lambda cell: arrived_ref.at[mine], arrived_ref, 1)

    all_bytes(card_ref, recv_sems.at[0]).wait()
    fastest = jnp.max(jnp.max(card_ref[:, pl.ds(0, 1), :], axis=0), axis=1, keepdims=True)
    timestep = jnp.broadcast_to(courant / (fastest + 1e-06), (blocks, particles))
    step_ref[...] = timestep

    name = myself.astype(jnp.float32)
    slot = lax.broadcasted_iota(jnp.int32, (blocks, particles), 0).astype(jnp.float32)
    count = jnp.zeros((1, particles), jnp.float32)
    own_start = jnp.zeros((1, particles), jnp.float32)
    goals = []
    list_ref[...] = jnp.zeros_like(list_ref)
    for cell, ranks in enumerate(ranks_all):
        target = cell_target(places, ranks, sizes)
        device = (target[0] * sizes[1] + target[1]) * sizes[2] + target[2]
        list_ref[pl.ds(cell, 1), :] = card_ref[device, pl.ds(GHOST_ROW, 1), :]
        own = jnp.where(mine == cell, 1.0, 0.0)
        own_start = own_start + own * count
        count = count + own * (blocks - MOVERS)
        for order in range(MOVERS):
            hit = card_ref[device, pl.ds(OWNER_ROW + order, 1), :] == name
            goals.append(jnp.where(hit, count, -1.0))
            count = count + jnp.where(hit, 1.0, 0.0)

    ids = list_ref[...]
    owners = jnp.floor((ids + 0.5) * (1.0 / blocks))
    wanted = owners == name
    lane_from = lax.broadcasted_iota(jnp.int32, (particles, particles), 0)
    lane_to = lax.broadcasted_iota(jnp.int32, (particles, particles), 1)
    earlier = jnp.where(lane_from < lane_to, 1.0, 0.0)
    ranked = jnp.dot(
        jnp.where(wanted, 1.0, 0.0), earlier, preferred_element_type=jnp.float32
    )
    for request in range(REQUESTS):
        fits = jnp.logical_and(wanted, jnp.abs(ranked - request) < 0.5)
        slots = jnp.sum(jnp.where(fits, ids - owners * blocks, 0.0), axis=1, keepdims=True)
        ask_ref[request] = jnp.broadcast_to(slots, ids.shape)

    all_bytes(arrived_ref, recv_sems.at[1]).wait()
    settled = [jnp.zeros((blocks, particles), jnp.float32) for _ in range(STATE)]
    for cell in range(cells):
        for order in range(MOVERS):
            chosen = slot == goals[cell * MOVERS + order]
            for comp in range(STATE):
                row = arrived_ref[cell, pl.ds(order * STATE + comp, 1), :]
                settled[comp] = jnp.where(chosen, row, settled[comp])
    stayed = jnp.int32(0)
    for block in range(blocks):
        stays = jnp.where(owner_ref[block] == myself, 1, 0)
        offset = jnp.where(stays == 1, stayed, -2 * blocks * MOVERS * cells).astype(jnp.float32)
        chosen = slot == own_start + offset
        for part, source in enumerate(sources):
            for dim in range(dims):
                comp = part * dims + dim
                row = source[dim, pl.ds(block, 1), :]
                settled[comp] = jnp.where(chosen, row, settled[comp])
        stayed += stays

    for dim in range(dims):
        halfway = settled[2 * dims + dim] + 0.5 * timestep * settled[3 * dims + dim]
        half_ref[dim] = halfway
        flat_ref[pl.ds(dim * blocks, blocks), :] = settled[dim]
        flat_ref[pl.ds((dims + dim) * blocks, blocks), :] = settled[dims + dim] + timestep * halfway
    comps = 2 * dims
    blocks_rows = []
    for block in range(blocks):
        rows = flat_ref[pl.ds(block, comps, stride=blocks), :]
        local_ref[block] = rows
        blocks_rows.append(rows)
    for cell in range(cells):
        for request in range(REQUESTS):
            ask = jnp.broadcast_to(ask_ref[request, pl.ds(cell, 1), :], (comps, particles))
            picked = blocks_rows[0]
            for block in range(1, blocks):
                picked = jnp.where(ask == block, blocks_rows[block], picked)
            pack_ref[cell, request] = picked

    for steps in steps_all:
        send_halo(steps, lambda cell: pack_ref.at[cell], ghosts_ref, 2)
    all_bytes(ghosts_ref, recv_sems.at[2]).wait()
    all_bytes(card_ref, send_sems.at[0]).wait()
    all_bytes(arrived_ref, send_sems.at[1]).wait()
    all_bytes(ghosts_ref, send_sems.at[2]).wait()


def exchange(sizes, new_owner, ghost_ids, ref_pos, displace, velocity, acceleration):
    dims, blocks, particles = ref_pos.shape
    cells = len(neighbour_steps(sizes)) + 1
    total = sizes[0] * sizes[1] * sizes[2]
    padded = -(-cells // SUBLANES) * SUBLANES
    ghosts = ghost_ids.astype(jnp.float32)[None]
    ghosts = jnp.pad(ghosts, ((0, 0), (0, particles - ghosts.shape[1])), constant_values=-blocks)
    smem = pl.BlockSpec(memory_space=pltpu.SMEM)
    vmem = pl.BlockSpec(memory_space=pltpu.VMEM)
    return pl.pallas_call(
        functools.partial(exchange_kernel, sizes),
        out_shape=(
            jax.ShapeDtypeStruct((blocks, 2 * dims, particles), jnp.float32),
            jax.ShapeDtypeStruct((cells, REQUESTS, 2 * dims, particles), jnp.float32),
            jax.ShapeDtypeStruct((dims, blocks, particles), jnp.float32),
            jax.ShapeDtypeStruct((blocks, particles), jnp.float32),
        ),
        in_specs=[smem, vmem, vmem, vmem, vmem, vmem],
        out_specs=(vmem, vmem, vmem, vmem),
        scratch_shapes=[
            pltpu.VMEM((cells, MOVERS * STATE, particles), jnp.float32),
            pltpu.VMEM((total, CARD, particles), jnp.float32),
            pltpu.VMEM((cells, REQUESTS, 2 * dims, particles), jnp.float32),
            pltpu.VMEM((padded, particles), jnp.float32),
            pltpu.VMEM((REQUESTS, padded, particles), jnp.float32),
            pltpu.VMEM((2 * dims * blocks, particles), jnp.float32),
            pltpu.SemaphoreType.DMA((3,)),
            pltpu.SemaphoreType.DMA((3,)),
        ],
        compiler_params=pltpu.CompilerParams(
            collective_id=0, has_side_effects=True, vmem_limit_bytes=16 * 1024 * 1024
        ),
    )(new_owner, ghosts, ref_pos, displace, velocity, acceleration)


def spread_away(index_ref, local_ref, ghosts_ref, rows_ref, turned_ref, order_ref, wide_ref):
    extended, comps, particles = rows_ref.shape
    blocks = local_ref.shape[0]
    batch = particles // comps
    used = local_ref.shape[1]
    aligned = SUBLANES * WORD_BITS
    groups = particles // SUBLANES
    rows_ref[...] = jnp.zeros_like(rows_ref)
    for block in range(blocks):
        rows_ref[block, pl.ds(0, used), :] = local_ref[block]
    for ghost in range(extended - blocks):
        rows_ref[blocks + ghost, pl.ds(0, used), :] = ghosts_ref[index_ref[ghost]]
    for part in range(extended // batch):
        rows = rows_ref[pl.ds(part * batch, batch)].reshape(particles, particles)
        turned_ref[...] = rows.T
        for step in range(groups):
            if step < WORD_BITS:
                column = turned_ref[pl.ds(step, SUBLANES, stride=WORD_BITS), :]
            else:
                start = aligned + (step - WORD_BITS) * SUBLANES
                column = turned_ref[pl.ds(start, SUBLANES), :]
            order_ref[part * groups + step] = column

    def spread_step(number, carry):
        part, step = number // groups, number % groups
        column = order_ref[number]
        for block in range(batch):
            for comp in range(used):
                place = block * comps + comp
                wide_ref[part * batch + block, step, comp] = jnp.broadcast_to(
                    column[:, place : place + 1], (SUBLANES, particles)
                )
        return carry

    lax.fori_loop(0, extended // batch * groups, spread_step, 0)


def tail_steps(particles):
    starts = range(SUBLANES * WORD_BITS, particles, SUBLANES)
    return [(start, start // WORD_BITS, (start + SUBLANES - 1) // WORD_BITS) for start in starts]


def tile_sum(home, away, front, back, wide_ref, bit_ref, particles):
    sublane = lax.broadcasted_iota(jnp.int32, (SUBLANES, particles), 0)
    sums = [jnp.zeros((SUBLANES, particles), jnp.float32) for _ in range(3)]
    tails = tail_steps(particles)
    for step in range(particles // SUBLANES):
        if step < WORD_BITS:
            hit = jnp.bitwise_and(front, 1 << step)
        else:
            start, low, high = tails[step - WORD_BITS]
            low, high = low - SUBLANES, high - SUBLANES
            row = jnp.broadcast_to(back[low : low + 1], (SUBLANES, particles))
            if high != low:
                upper = jnp.broadcast_to(back[high : high + 1], (SUBLANES, particles))
                row = jnp.where(sublane < (high + SUBLANES) * WORD_BITS - start, row, upper)
            hit = jnp.bitwise_and(row, bit_ref[step - WORD_BITS])
        other = [wide_ref[away, step, comp] for comp in range(6)]
        ref_gap = [other[k] - home[k] for k in range(3)]
        now_gap = [ref_gap[k] + (other[3 + k] - home[3 + k]) for k in range(3)]
        ref_sq = ref_gap[0] * ref_gap[0] + ref_gap[1] * ref_gap[1] + ref_gap[2] * ref_gap[2]
        now_sq = now_gap[0] * now_gap[0] + now_gap[1] * now_gap[1] + now_gap[2] * now_gap[2]
        scaled = jnp.where(hit != 0, lax.rsqrt(ref_sq) - lax.rsqrt(now_sq), 0.0)
        sums = [sums[k] + scaled * now_gap[k] for k in range(3)]
    return sums


def bond_kernel(
    words, pairs_ref, count_ref, index_ref, local_ref, ghosts_ref, half_ref, step_ref, bits_ref,
    displace_ref, velocity_ref, accel_ref,
    rows_ref, turned_ref, order_ref, wide_ref, total_ref, bit_ref,
):
    _, blocks, particles = accel_ref.shape
    pairs = bits_ref.shape[0] // words
    spread_away(index_ref, local_ref, ghosts_ref, rows_ref, turned_ref, order_ref, wide_ref)
    total_ref[...] = jnp.zeros_like(total_ref)
    sublane = lax.broadcasted_iota(jnp.int32, (SUBLANES, particles), 0)
    for number, (start, _, _) in enumerate(tail_steps(particles)):
        bit_ref[number] = jnp.left_shift(1, (sublane + start) % WORD_BITS)

    def not_own(first, rows):
        word = lax.broadcasted_iota(jnp.int32, (rows, particles), 0) + first
        lane = lax.broadcasted_iota(jnp.int32, (rows, particles), 1)
        own = jnp.where(lane // WORD_BITS == word, jnp.left_shift(1, lane % WORD_BITS), 0)
        return jnp.bitwise_not(own)

    behind = words - SUBLANES
    keep_front, keep_back = not_own(0, SUBLANES), not_own(SUBLANES, behind)
    count = count_ref[0]

    def pair_sums(wish):
        slot = jnp.minimum(wish, pairs - 1)
        live = jnp.where(wish < count, -1, 0)
        home_id = pairs_ref[0, slot]
        away_id = pairs_ref[1, slot]
        home = [
            jnp.broadcast_to(rows_ref[home_id, pl.ds(comp, 1), :], (SUBLANES, particles))
            for comp in range(6)
        ]
        apart = jnp.where(home_id == away_id, 0, -1)
        front = bits_ref[pl.ds(slot, SUBLANES, stride=pairs), :]
        back = bits_ref[pl.ds(slot + SUBLANES * pairs, behind, stride=pairs), :]
        front = front & ((keep_front | apart) & live)
        back = back & ((keep_back | apart) & live)
        return home_id, tile_sum(home, away_id, front, back, wide_ref, bit_ref, particles)

    def add_pairs(number, carry):
        found = [pair_sums(number * TOGETHER + order) for order in range(TOGETHER)]
        for home_id, sums in found:
            for comp in range(3):
                total_ref[home_id, comp] += sums[comp]
        return carry

    lax.fori_loop(0, (count + TOGETHER - 1) // TOGETHER, add_pairs, 0)
    accel = stiffness * jnp.sum(total_ref[...], axis=2)
    for comp in range(3):
        for block in range(blocks):
            accel_ref[comp, pl.ds(block, 1), :] = accel[block, comp : comp + 1]
            displace_ref[comp, pl.ds(block, 1), :] = local_ref[block, pl.ds(3 + comp, 1), :]
        velocity_ref[comp] = half_ref[comp] + 0.5 * step_ref[...] * accel_ref[comp]


def bond_step(index, local, ghosts, half, step, pair_blocks, pair_count, bond_bits):
    blocks, particles = step.shape
    extended = index.shape[0] + blocks
    words, pairs = bond_bits.shape[0:2]
    shape = jax.ShapeDtypeStruct((3, blocks, particles), jnp.float32)
    smem = pl.BlockSpec(memory_space=pltpu.SMEM)
    vmem = pl.BlockSpec(memory_space=pltpu.VMEM)
    groups = particles // SUBLANES
    return pl.pallas_call(
        functools.partial(bond_kernel, words),
        out_shape=(shape, shape, shape),
        in_specs=[smem, smem, smem, vmem, vmem, vmem, vmem, vmem],
        out_specs=(vmem, vmem, vmem),
        scratch_shapes=[
            pltpu.VMEM((extended, SUBLANES, particles), jnp.float32),
            pltpu.VMEM((particles, particles), jnp.float32),
            pltpu.VMEM((extended * SUBLANES // particles * groups, SUBLANES, particles), jnp.float32),
            pltpu.VMEM((extended, groups, 6, SUBLANES, particles), jnp.float32),
            pltpu.VMEM((blocks, 3, SUBLANES, particles), jnp.float32),
            pltpu.VMEM((len(tail_steps(particles)), SUBLANES, particles), jnp.int32),
        ],
        compiler_params=pltpu.CompilerParams(vmem_limit_bytes=40 * 1024 * 1024),
    )(pair_blocks, pair_count, index, local, ghosts, half, step, bond_bits.reshape(words * pairs, particles))


def per_device(
    ref_pos,
    displace,
    velocity,
    acceleration,
    new_owner,
    ghost_ids,
    pair_blocks,
    pair_count,
    bond_bits,
):
    blocks = ref_pos.shape[0]
    sizes = tuple(lax.axis_size(name) for name in AXES)
    places = [lax.axis_index(name) for name in AXES]
    turned = [array.transpose(1, 0, 2) for array in (ref_pos, displace, velocity, acceleration)]
    local, ghosts, half, step = exchange(sizes, new_owner, ghost_ids, *turned)
    ghost_dev = ghost_ids // blocks
    ghost_places = (
        ghost_dev // (sizes[1] * sizes[2]),
        ghost_dev // sizes[2] % sizes[1],
        ghost_dev % sizes[2],
    )
    moves = []
    for ghost, place, size in zip(ghost_places, places, sizes):
        apart = (ghost - place) % size
        moves.append(jnp.where(apart == size - 1, -1, apart) if size > 2 else apart)
    ghost_cell = cell_of(places, moves, sizes)
    order = jnp.arange(ghost_ids.shape[0])
    repeats = (ghost_dev[:, None] == ghost_dev[None, :]) & (order[None, :] < order[:, None])
    index = ghost_cell * REQUESTS + jnp.sum(repeats.astype(jnp.int32), axis=1)
    ghosts = ghosts.reshape((-1,) + ghosts.shape[2:])
    results = bond_step(
        index, local, ghosts, half, step, pair_blocks, pair_count, bond_bits.transpose(1, 0, 2)
    )
    return tuple(array.transpose(1, 0, 2) for array in results)


def solution(mesh):
    in_specs = (
        P(("gx", "gy", "gz"), None, None),
        P(("gx", "gy", "gz"), None, None),
        P(("gx", "gy", "gz"), None, None),
        P(("gx", "gy", "gz"), None, None),
        P(("gx", "gy", "gz")),
        P(("gx", "gy", "gz")),
        P(None, ("gx", "gy", "gz")),
        P(("gx", "gy", "gz")),
        P(("gx", "gy", "gz"), None, None),
    )
    out_specs = (
        P(("gx", "gy", "gz"), None, None),
        P(("gx", "gy", "gz"), None, None),
        P(("gx", "gy", "gz"), None, None),
    )
    return jax.shard_map(
        per_device, mesh=mesh, in_specs=in_specs, out_specs=out_specs, check_vma=False
    )
```

```python
import functools

import jax
import jax.numpy as jnp
from jax import lax
from jax.experimental import pallas as pl
from jax.experimental.pallas import tpu as pltpu
from jax.sharding import PartitionSpec as P

WORD_BITS = 11


courant = 0.05
stiffness = 20.0


MESH = pl.DeviceIdType.MESH
AXES = ("gx", "gy", "gz")
MOVERS = 2
REQUESTS = 3
STATE = 12
SUBLANES = 8
OWNER_ROW = 1
GHOST_ROW = OWNER_ROW + MOVERS
CARD = GHOST_ROW + 1
UNROLLED = 64
TOGETHER = 2


def reach(size):
    return (0,) if size == 1 else (0, 1) if size == 2 else (-1, 0, 1)


def cell_rank(place, step, size):
    if size < 3:
        return (place + step) % size
    first = (size - place) // size
    last = (place + 1) // size
    return (step + 1 + 2 * first + last) % 3


def cell_of(places, steps, sizes):
    cell = 0
    for place, step, size in zip(places, steps, sizes):
        cell = cell * len(reach(size)) + cell_rank(place, step, size)
    return cell


def neighbour_steps(sizes):
    every = [(x, y, z) for x in reach(sizes[0]) for y in reach(sizes[1]) for z in reach(sizes[2])]
    return [steps for steps in every if steps != (0, 0, 0)]


def cell_target(places, ranks, sizes):
    target = []
    for place, rank, size in zip(places, ranks, sizes):
        if size < 3:
            target.append(jnp.int32(rank))
        else:
            first = (size - place) // size
            last = (place + 1) // size
            target.append((place + (rank + 6 - 2 * first - last) % 3 - 1 + size) % size)
    return target


def exchange_kernel(
    sizes,
    owner_in, ghost_in, ref_in, disp_in, vel_in, acc_in,
    ext_ref, half_ref, step_ref,
    owner_ref, ghost_ref, ref_ref, disp_ref, vel_ref, acc_ref,
    arrived_ref, card_ref, pack_ref, ghosts_ref, list_ref, ask_ref, flat_ref,
    send_sems, recv_sems, load_sems,
):
    dims, blocks, particles = ref_ref.shape
    inner = (owner_ref, ghost_ref, ref_ref, disp_ref, vel_ref, acc_ref)
    outer = (owner_in, ghost_in, ref_in, disp_in, vel_in, acc_in)
    loads = [
        pltpu.make_async_copy(source, target, load_sems.at[number])
        for number, (source, target) in enumerate(zip(outer, inner))
    ]
    for load in loads:
        load.start()
    total = sizes[0] * sizes[1] * sizes[2]
    steps_all = neighbour_steps(sizes)
    cells = len(steps_all) + 1
    extents = [len(reach(size)) for size in sizes]
    ranks_all = [
        (x, y, z) for x in range(extents[0]) for y in range(extents[1]) for z in range(extents[2])
    ]
    places = [lax.axis_index(name) for name in AXES]
    myself = (places[0] * sizes[1] + places[1]) * sizes[2] + places[2]
    mine = cell_of(places, (0, 0, 0), sizes)
    sources = (ref_ref, disp_ref, vel_ref, acc_ref)

    def to_others(action):
        if total <= UNROLLED:
            coords = [
                [(place + step) % size for step in range(size)]
                for place, size in zip(places, sizes)
            ]
            for x in range(sizes[0]):
                for y in range(sizes[1]):
                    for z in range(sizes[2]):
                        if (x, y, z) != (0, 0, 0):
                            action((coords[0][x], coords[1][y], coords[2][z]))
        else:

            def act(number, carry):
                device = (myself + number) % total
                rest = device // sizes[2]
                action((rest // sizes[1], rest % sizes[1], device % sizes[2]))
                return carry

            lax.fori_loop(1, total, act, 0)

    barrier = pltpu.get_barrier_semaphore()
    to_others(
        lambda target: pl.semaphore_signal(barrier, inc=1, device_id=target, device_id_type=MESH)
    )

    for load in loads:
        load.wait()
    leavers = [jnp.int32(0) for _ in range(MOVERS)]
    seen = jnp.int32(0)
    for block in range(blocks):
        leaves = jnp.where(owner_ref[block] != myself, 1, 0)
        for order in range(MOVERS):
            leavers[order] += block * leaves * jnp.where(seen == order, 1, 0)
        seen += leaves
    speeds = jnp.max(jnp.abs(vel_ref[...]), axis=0)
    card_ref[myself, pl.ds(0, 1), :] = jnp.max(speeds, axis=0, keepdims=True)
    for order in range(MOVERS):
        owner = jnp.full((1, particles), owner_ref[leavers[order]], jnp.int32)
        card_ref[myself, pl.ds(OWNER_ROW + order, 1), :] = owner.astype(jnp.float32)
    ghosts = ghost_ref.shape[0]
    lane = lax.broadcasted_iota(jnp.int32, (1, particles), 1)
    wish = jnp.full((1, particles), -blocks, jnp.int32)
    for ghost in range(ghosts):
        wish = jnp.where(lane == ghost, ghost_ref[ghost], wish)
    card_ref[myself, pl.ds(GHOST_ROW, 1), :] = wish.astype(jnp.float32)
    for order in range(MOVERS):
        for part, source in enumerate(sources):
            for dim in range(dims):
                row = order * STATE + part * dims + dim
                arrived_ref[mine, pl.ds(row, 1), :] = source[dim, pl.ds(leavers[order], 1), :]

    pl.semaphore_wait(barrier, total - 1)

    def send_card(target):
        pltpu.make_async_remote_copy(
            src_ref=card_ref.at[myself],
            dst_ref=card_ref.at[myself],
            send_sem=send_sems.at[0],
            recv_sem=recv_sems.at[0],
            device_id=target,
            device_id_type=MESH,
        ).start()

    def send_halo(steps, source_of, ref, kind):
        target = [(place + step) % size for place, step, size in zip(places, steps, sizes)]
        back = [-step for step in steps]
        pltpu.make_async_remote_copy(
            src_ref=source_of(cell_of(places, steps, sizes)),
            dst_ref=ref.at[cell_of(target, back, sizes)],
            send_sem=send_sems.at[kind],
            recv_sem=recv_sems.at[kind],
            device_id=tuple(target),
            device_id_type=MESH,
        ).start()

    def all_bytes(ref, sem):
        part = ref.at[pl.ds(0, ref.shape[0] - 1)]
        return pltpu.make_async_copy(part, part, sem)

    to_others(send_card)
    for steps in steps_all:
        send_halo(steps, lambda cell: arrived_ref.at[mine], arrived_ref, 1)

    all_bytes(card_ref, recv_sems.at[0]).wait()
    fastest = jnp.max(jnp.max(card_ref[:, pl.ds(0, 1), :], axis=0), axis=1, keepdims=True)
    timestep = jnp.broadcast_to(courant / (fastest + 1e-06), (blocks, particles))
    step_ref[...] = timestep

    name = myself.astype(jnp.float32)
    slot = lax.broadcasted_iota(jnp.int32, (blocks, particles), 0).astype(jnp.float32)
    count = jnp.zeros((1, particles), jnp.float32)
    own_start = jnp.zeros((1, particles), jnp.float32)
    goals = []
    list_ref[...] = jnp.zeros_like(list_ref)
    for cell, ranks in enumerate(ranks_all):
        target = cell_target(places, ranks, sizes)
        device = (target[0] * sizes[1] + target[1]) * sizes[2] + target[2]
        list_ref[pl.ds(cell, 1), :] = card_ref[device, pl.ds(GHOST_ROW, 1), :]
        own = jnp.where(mine == cell, 1.0, 0.0)
        own_start = own_start + own * count
        count = count + own * (blocks - MOVERS)
        for order in range(MOVERS):
            hit = card_ref[device, pl.ds(OWNER_ROW + order, 1), :] == name
            goals.append(jnp.where(hit, count, -1.0))
            count = count + jnp.where(hit, 1.0, 0.0)

    ids = list_ref[...]
    owners = jnp.floor((ids + 0.5) * (1.0 / blocks))
    wanted = owners == name
    lane_from = lax.broadcasted_iota(jnp.int32, (particles, particles), 0)
    lane_to = lax.broadcasted_iota(jnp.int32, (particles, particles), 1)
    earlier = jnp.where(lane_from < lane_to, 1.0, 0.0)
    ranked = jnp.dot(
        jnp.where(wanted, 1.0, 0.0), earlier, preferred_element_type=jnp.float32
    )
    for request in range(REQUESTS):
        fits = jnp.logical_and(wanted, jnp.abs(ranked - request) < 0.5)
        slots = jnp.sum(jnp.where(fits, ids - owners * blocks, 0.0), axis=1, keepdims=True)
        ask_ref[request] = jnp.broadcast_to(slots, ids.shape)

    all_bytes(arrived_ref, recv_sems.at[1]).wait()
    settled = [jnp.zeros((blocks, particles), jnp.float32) for _ in range(STATE)]
    for cell in range(cells):
        for order in range(MOVERS):
            chosen = slot == goals[cell * MOVERS + order]
            for comp in range(STATE):
                row = arrived_ref[cell, pl.ds(order * STATE + comp, 1), :]
                settled[comp] = jnp.where(chosen, row, settled[comp])
    stayed = jnp.int32(0)
    for block in range(blocks):
        stays = jnp.where(owner_ref[block] == myself, 1, 0)
        offset = jnp.where(stays == 1, stayed, -2 * blocks * MOVERS * cells).astype(jnp.float32)
        chosen = slot == own_start + offset
        for part, source in enumerate(sources):
            for dim in range(dims):
                comp = part * dims + dim
                row = source[dim, pl.ds(block, 1), :]
                settled[comp] = jnp.where(chosen, row, settled[comp])
        stayed += stays

    for dim in range(dims):
        halfway = settled[2 * dims + dim] + 0.5 * timestep * settled[3 * dims + dim]
        half_ref[dim] = halfway
        flat_ref[pl.ds(dim * blocks, blocks), :] = settled[dim]
        flat_ref[pl.ds((dims + dim) * blocks, blocks), :] = settled[dims + dim] + timestep * halfway
    comps = 2 * dims
    blocks_rows = []
    for block in range(blocks):
        rows = flat_ref[pl.ds(block, comps, stride=blocks), :]
        ext_ref[block] = jnp.zeros((SUBLANES, particles), jnp.float32)
        ext_ref[block, pl.ds(0, comps), :] = rows
        blocks_rows.append(rows)
    for cell in range(cells):
        for request in range(REQUESTS):
            ask = jnp.broadcast_to(ask_ref[request, pl.ds(cell, 1), :], (comps, particles))
            picked = blocks_rows[0]
            for block in range(1, blocks):
                picked = jnp.where(ask == block, blocks_rows[block], picked)
            pack_ref[cell, request] = picked

    for steps in steps_all:
        send_halo(steps, lambda cell: pack_ref.at[cell], ghosts_ref, 2)
    taken = []
    for ghost in range(ghosts):
        device = lax.div(ghost_ref[ghost], blocks)
        rest = lax.div(device, sizes[2])
        spots = (lax.div(rest, sizes[1]), lax.rem(rest, sizes[1]), lax.rem(device, sizes[2]))
        moves = []
        for spot, place, size in zip(spots, places, sizes):
            apart = lax.rem(spot - place + size, size)
            moves.append(jnp.where(apart == size - 1, -1, apart) if size > 2 else apart)
        repeats = jnp.int32(0)
        for _, before in taken:
            repeats += jnp.where(before == device, 1, 0)
        taken.append((cell_of(places, moves, sizes) * REQUESTS + repeats, device))
    for ghost in range(ghosts):
        ext_ref[blocks + ghost] = jnp.zeros((SUBLANES, particles), jnp.float32)
    all_bytes(ghosts_ref, recv_sems.at[2]).wait()
    for ghost, (index, _) in enumerate(taken):
        rows = ghosts_ref[lax.div(index, REQUESTS), lax.rem(index, REQUESTS)]
        ext_ref[blocks + ghost, pl.ds(0, comps), :] = rows
    all_bytes(card_ref, send_sems.at[0]).wait()
    all_bytes(arrived_ref, send_sems.at[1]).wait()
    all_bytes(ghosts_ref, send_sems.at[2]).wait()


def exchange(sizes, new_owner, ghost_ids, ref_pos, displace, velocity, acceleration):
    dims, blocks, particles = ref_pos.shape
    cells = len(neighbour_steps(sizes)) + 1
    total = sizes[0] * sizes[1] * sizes[2]
    padded = -(-cells // SUBLANES) * SUBLANES
    ghosts = ghost_ids.shape[0]
    hbm = pl.BlockSpec(memory_space=pltpu.HBM)
    vmem = pl.BlockSpec(memory_space=pltpu.VMEM)
    return pl.pallas_call(
        functools.partial(exchange_kernel, sizes),
        out_shape=(
            jax.ShapeDtypeStruct((blocks + ghosts, SUBLANES, particles), jnp.float32),
            jax.ShapeDtypeStruct((dims, blocks, particles), jnp.float32),
            jax.ShapeDtypeStruct((blocks, particles), jnp.float32),
        ),
        in_specs=[hbm] * 6,
        out_specs=(vmem, vmem, vmem),
        scratch_shapes=[
            pltpu.SMEM(new_owner.shape, jnp.int32),
            pltpu.SMEM(ghost_ids.shape, jnp.int32),
            pltpu.VMEM(ref_pos.shape, jnp.float32),
            pltpu.VMEM(ref_pos.shape, jnp.float32),
            pltpu.VMEM(ref_pos.shape, jnp.float32),
            pltpu.VMEM(ref_pos.shape, jnp.float32),
            pltpu.VMEM((cells, MOVERS * STATE, particles), jnp.float32),
            pltpu.VMEM((total, CARD, particles), jnp.float32),
            pltpu.VMEM((cells, REQUESTS, 2 * dims, particles), jnp.float32),
            pltpu.VMEM((cells, REQUESTS, 2 * dims, particles), jnp.float32),
            pltpu.VMEM((padded, particles), jnp.float32),
            pltpu.VMEM((REQUESTS, padded, particles), jnp.float32),
            pltpu.VMEM((2 * dims * blocks, particles), jnp.float32),
            pltpu.SemaphoreType.DMA((3,)),
            pltpu.SemaphoreType.DMA((3,)),
            pltpu.SemaphoreType.DMA((6,)),
        ],
        compiler_params=pltpu.CompilerParams(
            collective_id=0, has_side_effects=True, vmem_limit_bytes=16 * 1024 * 1024
        ),
    )(new_owner, ghost_ids, ref_pos, displace, velocity, acceleration)


def spread_away(ext_ref, rows_ref, turned_ref, sorted_ref, mask_ref, ones_ref, wide_ref):
    extended, comps, particles = ext_ref.shape
    used = wide_ref.shape[1]
    groups = wide_ref.shape[2]
    halves = sorted_ref.shape[0]
    stride = 4 * comps
    batch = particles // stride
    aligned = SUBLANES * WORD_BITS
    rows_ref[...] = jnp.zeros_like(rows_ref)
    for block in range(extended):
        rest = ext_ref[block]
        for term in range(3):
            part = rest.astype(jnp.bfloat16).astype(jnp.float32)
            rows_ref[pl.ds(block * stride + term * comps, comps), :] = part
            rest = rest - part
    for number in range(2 * halves):
        turned_ref[number] = rows_ref[pl.ds(number * particles, particles), :].T
    for number in range(2 * halves):
        half, column = number % halves, number // halves * particles
        for pair in range(groups // 2):
            parts = []
            for step in (2 * pair, 2 * pair + 1):
                if step < WORD_BITS:
                    parts.append(turned_ref[number, pl.ds(step, SUBLANES, stride=WORD_BITS), :])
                else:
                    start = aligned + (step - WORD_BITS) * SUBLANES
                    parts.append(turned_ref[number, pl.ds(start, SUBLANES), :])
            both = jnp.concatenate(parts, axis=0).astype(jnp.bfloat16)
            sorted_ref[half, pair, :, pl.ds(column, particles)] = both
    lane = lax.broadcasted_iota(jnp.int32, mask_ref.shape[2:], 1) % particles
    for block in range(batch):
        for comp in range(used):
            keep = jnp.logical_and(lane // stride == block, lane % comps == comp)
            mask_ref[block, comp] = jnp.where(keep, 1.0, 0.0).astype(jnp.bfloat16)
    above = lax.broadcasted_iota(jnp.int32, ones_ref.shape, 0) // particles
    beside = lax.broadcasted_iota(jnp.int32, ones_ref.shape, 1) // particles
    ones_ref[...] = jnp.where(above == beside, 1.0, 0.0).astype(jnp.bfloat16)

    def spread_half(half, carry):
        table = sorted_ref[half]
        for block in range(batch):
            kept = [
                (table * mask_ref[block, comp][None]).reshape(particles, 2 * particles)
                for comp in range(used)
            ]
            spread = jnp.dot(
                jnp.concatenate(kept, axis=0), ones_ref[...], preferred_element_type=jnp.float32
            )
            for side in range(2):
                part = spread[:, side * particles : (side + 1) * particles]
                place = (half + side * halves) * batch + block
                wide_ref[place] = part.reshape(used, groups, SUBLANES, particles)
        return carry

    lax.fori_loop(0, halves, spread_half, 0)


def tail_steps(particles):
    starts = range(SUBLANES * WORD_BITS, particles, SUBLANES)
    return [(start, start // WORD_BITS, (start + SUBLANES - 1) // WORD_BITS) for start in starts]


def tile_sum(home, away, front, back, wide_ref, bit_ref, particles):
    sublane = lax.broadcasted_iota(jnp.int32, (SUBLANES, particles), 0)
    sums = [jnp.zeros((SUBLANES, particles), jnp.float32) for _ in range(3)]
    tails = tail_steps(particles)
    for step in range(particles // SUBLANES):
        if step < WORD_BITS:
            hit = jnp.bitwise_and(front, 1 << step)
        else:
            start, low, high = tails[step - WORD_BITS]
            low, high = low - SUBLANES, high - SUBLANES
            row = jnp.broadcast_to(back[low : low + 1], (SUBLANES, particles))
            if high != low:
                upper = jnp.broadcast_to(back[high : high + 1], (SUBLANES, particles))
                row = jnp.where(sublane < (high + SUBLANES) * WORD_BITS - start, row, upper)
            hit = jnp.bitwise_and(row, bit_ref[step - WORD_BITS])
        other = [wide_ref[away, comp, step] for comp in range(6)]
        ref_gap = [other[k] - home[k] for k in range(3)]
        now_gap = [ref_gap[k] + (other[3 + k] - home[3 + k]) for k in range(3)]
        ref_sq = ref_gap[0] * ref_gap[0] + ref_gap[1] * ref_gap[1] + ref_gap[2] * ref_gap[2]
        now_sq = now_gap[0] * now_gap[0] + now_gap[1] * now_gap[1] + now_gap[2] * now_gap[2]
        scaled = jnp.where(hit != 0, lax.rsqrt(ref_sq) - lax.rsqrt(now_sq), 0.0)
        sums = [sums[k] + scaled * now_gap[k] for k in range(3)]
    return sums


def bond_kernel(
    words, pairs_in, bits_in, count_ref, ext_ref, half_ref, step_ref,
    displace_ref, velocity_ref, accel_ref,
    pairs_ref, bits_ref, rows_ref, turned_ref, sorted_ref, mask_ref, ones_ref, wide_ref,
    total_ref, bit_ref, load_sems,
):
    _, blocks, particles = accel_ref.shape
    pairs = bits_ref.shape[0] // words
    loads = [
        pltpu.make_async_copy(pairs_in, pairs_ref, load_sems.at[0]),
        pltpu.make_async_copy(bits_in, bits_ref, load_sems.at[1]),
    ]
    for load in loads:
        load.start()
    spread_away(ext_ref, rows_ref, turned_ref, sorted_ref, mask_ref, ones_ref, wide_ref)
    total_ref[...] = jnp.zeros_like(total_ref)
    sublane = lax.broadcasted_iota(jnp.int32, (SUBLANES, particles), 0)
    for number, (start, _, _) in enumerate(tail_steps(particles)):
        bit_ref[number] = jnp.left_shift(1, (sublane + start) % WORD_BITS)

    def not_own(first, rows):
        word = lax.broadcasted_iota(jnp.int32, (rows, particles), 0) + first
        lane = lax.broadcasted_iota(jnp.int32, (rows, particles), 1)
        own = jnp.where(lane // WORD_BITS == word, jnp.left_shift(1, lane % WORD_BITS), 0)
        return jnp.bitwise_not(own)

    behind = words - SUBLANES
    keep_front, keep_back = not_own(0, SUBLANES), not_own(SUBLANES, behind)
    count = count_ref[0]
    for load in loads:
        load.wait()

    def pair_sums(wish):
        slot = jnp.minimum(wish, pairs - 1)
        live = jnp.where(wish < count, -1, 0)
        home_id = pairs_ref[0, slot]
        away_id = pairs_ref[1, slot]
        home = [
            jnp.broadcast_to(ext_ref[home_id, pl.ds(comp, 1), :], (SUBLANES, particles))
            for comp in range(6)
        ]
        apart = jnp.where(home_id == away_id, 0, -1)
        front = bits_ref[pl.ds(slot, SUBLANES, stride=pairs), :]
        back = bits_ref[pl.ds(slot + SUBLANES * pairs, behind, stride=pairs), :]
        front = front & ((keep_front | apart) & live)
        back = back & ((keep_back | apart) & live)
        return home_id, tile_sum(home, away_id, front, back, wide_ref, bit_ref, particles)

    def add_pairs(number, carry):
        found = [pair_sums(number * TOGETHER + order) for order in range(TOGETHER)]
        for home_id, sums in found:
            for comp in range(3):
                total_ref[home_id, comp] += sums[comp]
        return carry

    lax.fori_loop(0, (count + TOGETHER - 1) // TOGETHER, add_pairs, 0)
    accel = stiffness * jnp.sum(total_ref[...], axis=2)
    for comp in range(3):
        for block in range(blocks):
            accel_ref[comp, pl.ds(block, 1), :] = accel[block, comp : comp + 1]
            displace_ref[comp, pl.ds(block, 1), :] = ext_ref[block, pl.ds(3 + comp, 1), :]
        velocity_ref[comp] = half_ref[comp] + 0.5 * step_ref[...] * accel_ref[comp]


def bond_step(ext, half, step, pair_blocks, pair_count, bond_bits):
    blocks, particles = step.shape
    extended = ext.shape[0]
    words, pairs = bond_bits.shape[0:2]
    shape = jax.ShapeDtypeStruct((3, blocks, particles), jnp.float32)
    smem = pl.BlockSpec(memory_space=pltpu.SMEM)
    vmem = pl.BlockSpec(memory_space=pltpu.VMEM)
    hbm = pl.BlockSpec(memory_space=pltpu.HBM)
    groups = particles // SUBLANES
    batch = particles // (4 * SUBLANES)
    halves = -(-extended // (2 * batch))
    return pl.pallas_call(
        functools.partial(bond_kernel, words),
        out_shape=(shape, shape, shape),
        in_specs=[hbm, hbm, smem, vmem, vmem, vmem],
        out_specs=(vmem, vmem, vmem),
        scratch_shapes=[
            pltpu.SMEM(pair_blocks.shape, jnp.int32),
            pltpu.VMEM((words * pairs, particles), jnp.int32),
            pltpu.VMEM((2 * halves * particles, particles), jnp.float32),
            pltpu.VMEM((2 * halves, particles, particles), jnp.float32),
            pltpu.VMEM((halves, groups // 2, 2 * SUBLANES, 2 * particles), jnp.bfloat16),
            pltpu.VMEM((batch, 6, 2 * SUBLANES, 2 * particles), jnp.bfloat16),
            pltpu.VMEM((2 * particles, 2 * particles), jnp.bfloat16),
            pltpu.VMEM((2 * halves * batch, 6, groups, SUBLANES, particles), jnp.float32),
            pltpu.VMEM((blocks, 3, SUBLANES, particles), jnp.float32),
            pltpu.VMEM((len(tail_steps(particles)), SUBLANES, particles), jnp.int32),
            pltpu.SemaphoreType.DMA((2,)),
        ],
        compiler_params=pltpu.CompilerParams(vmem_limit_bytes=40 * 1024 * 1024),
    )(pair_blocks, bond_bits.reshape(words * pairs, particles), pair_count, ext, half, step)


def per_device(
    ref_pos,
    displace,
    velocity,
    acceleration,
    new_owner,
    ghost_ids,
    pair_blocks,
    pair_count,
    bond_bits,
):
    sizes = tuple(lax.axis_size(name) for name in AXES)
    turned = [array.transpose(1, 0, 2) for array in (ref_pos, displace, velocity, acceleration)]
    ext, half, step = exchange(sizes, new_owner, ghost_ids, *turned)
    results = bond_step(ext, half, step, pair_blocks, pair_count, bond_bits.transpose(1, 0, 2))
    return tuple(array.transpose(1, 0, 2) for array in results)


def solution(mesh):
    in_specs = (
        P(("gx", "gy", "gz"), None, None),
        P(("gx", "gy", "gz"), None, None),
        P(("gx", "gy", "gz"), None, None),
        P(("gx", "gy", "gz"), None, None),
        P(("gx", "gy", "gz")),
        P(("gx", "gy", "gz")),
        P(None, ("gx", "gy", "gz")),
        P(("gx", "gy", "gz")),
        P(("gx", "gy", "gz"), None, None),
    )
    out_specs = (
        P(("gx", "gy", "gz"), None, None),
        P(("gx", "gy", "gz"), None, None),
        P(("gx", "gy", "gz"), None, None),
    )
    return jax.shard_map(
        per_device, mesh=mesh, in_specs=in_specs, out_specs=out_specs, check_vma=False
    )
```

```python
import functools

import jax
import jax.numpy as jnp
from jax import lax
from jax.experimental import pallas as pl
from jax.experimental.pallas import tpu as pltpu
from jax.sharding import PartitionSpec as P

WORD_BITS = 11


courant = 0.05
stiffness = 20.0


MESH = pl.DeviceIdType.MESH
AXES = ("gx", "gy", "gz")
MOVERS = 2
REQUESTS = 3
STATE = 12
SUBLANES = 8
OWNER_ROW = 1
GHOST_ROW = OWNER_ROW + MOVERS
CARD = GHOST_ROW + 1
UNROLLED = 64
TOGETHER = 2


def reach(size):
    return (0,) if size == 1 else (0, 1) if size == 2 else (-1, 0, 1)


def cell_rank(place, step, size):
    if size < 3:
        return (place + step) % size
    first = (size - place) // size
    last = (place + 1) // size
    return (step + 1 + 2 * first + last) % 3


def cell_of(places, steps, sizes):
    cell = 0
    for place, step, size in zip(places, steps, sizes):
        cell = cell * len(reach(size)) + cell_rank(place, step, size)
    return cell


def neighbour_steps(sizes):
    every = [(x, y, z) for x in reach(sizes[0]) for y in reach(sizes[1]) for z in reach(sizes[2])]
    return [steps for steps in every if steps != (0, 0, 0)]


def exchange_kernel(
    sizes,
    owner_in, ghost_in, ref_in, disp_in, vel_in, acc_in,
    ext_out, half_out, step_out,
    owner_ref, ghost_ref, ref_ref, disp_ref, vel_ref, acc_ref,
    arrived_ref, card_ref, peak_ref, pack_ref, ghosts_ref, list_ref, ask_ref, flat_ref,
    ext_ref, half_ref, step_ref,
    send_sems, recv_sems, load_sems, store_sems,
):
    dims, blocks, particles = ref_ref.shape
    inner = (owner_ref, ghost_ref, ref_ref, disp_ref, vel_ref, acc_ref)
    outer = (owner_in, ghost_in, ref_in, disp_in, vel_in, acc_in)
    loads = [
        pltpu.make_async_copy(source, target, load_sems.at[number])
        for number, (source, target) in enumerate(zip(outer, inner))
    ]
    for load in loads:
        load.start()
    total = sizes[0] * sizes[1] * sizes[2]
    steps_all = sorted(neighbour_steps(sizes), key=lambda steps: -abs(steps[0]))
    cells = len(steps_all) + 1
    far = total - cells if total <= UNROLLED else total - 1
    places = [lax.axis_index(name) for name in AXES]
    myself = (places[0] * sizes[1] + places[1]) * sizes[2] + places[2]
    mine = cell_of(places, (0, 0, 0), sizes)
    routes = {}
    for steps in steps_all:
        target = [(place + step) % size for place, step, size in zip(places, steps, sizes)]
        back = [-step for step in steps]
        routes[steps] = (
            tuple(target), cell_of(places, steps, sizes), cell_of(target, back, sizes)
        )
    sources = (ref_ref, disp_ref, vel_ref, acc_ref)

    def to_others(action, near):
        if total <= UNROLLED:
            coords = [
                [(place + step) % size for step in range(size)]
                for place, size in zip(places, sizes)
            ]
            for x in range(sizes[0]):
                for y in range(sizes[1]):
                    for z in range(sizes[2]):
                        wraps = zip((x, y, z), sizes)
                        beside = all(step in (0, 1, size - 1) for step, size in wraps)
                        if (x, y, z) != (0, 0, 0) and (near or not beside):
                            action((coords[0][x], coords[1][y], coords[2][z]))
        else:

            def act(number, carry):
                device = (myself + number) % total
                rest = device // sizes[2]
                action((rest // sizes[1], rest % sizes[1], device % sizes[2]))
                return carry

            lax.fori_loop(1, total, act, 0)

    peak_ref[...] = jnp.zeros_like(peak_ref)
    barrier = pltpu.get_barrier_semaphore()
    to_others(
        lambda target: pl.semaphore_signal(barrier, inc=1, device_id=target, device_id_type=MESH),
        True,
    )

    for load in loads:
        load.wait()
    leavers = [jnp.int32(0) for _ in range(MOVERS)]
    seen = jnp.int32(0)
    for block in range(blocks):
        leaves = jnp.where(owner_ref[block] != myself, 1, 0)
        for order in range(MOVERS):
            leavers[order] += block * leaves * jnp.where(seen == order, 1, 0)
        seen += leaves
    speeds = jnp.max(jnp.abs(vel_ref[...]), axis=0)
    peak = jnp.max(speeds, axis=0, keepdims=True)
    card_ref[mine, pl.ds(0, 1), :] = peak
    peak_ref[myself] = peak
    for order in range(MOVERS):
        owner = jnp.full((1, particles), owner_ref[leavers[order]], jnp.int32)
        card_ref[mine, pl.ds(OWNER_ROW + order, 1), :] = owner.astype(jnp.float32)
    ghosts = ghost_ref.shape[0]
    lane = lax.broadcasted_iota(jnp.int32, (1, particles), 1)
    wish = jnp.full((1, particles), -blocks, jnp.int32)
    for ghost in range(ghosts):
        wish = jnp.where(lane == ghost, ghost_ref[ghost], wish)
    card_ref[mine, pl.ds(GHOST_ROW, 1), :] = wish.astype(jnp.float32)
    for order in range(MOVERS):
        for part, source in enumerate(sources):
            for dim in range(dims):
                row = order * STATE + part * dims + dim
                arrived_ref[mine, pl.ds(row, 1), :] = source[dim, pl.ds(leavers[order], 1), :]

    pl.semaphore_wait(barrier, total - 1)

    def send_peak(target):
        pltpu.make_async_remote_copy(
            src_ref=peak_ref.at[myself],
            dst_ref=peak_ref.at[myself],
            send_sem=send_sems.at[3],
            recv_sem=recv_sems.at[3],
            device_id=target,
            device_id_type=MESH,
        ).start()

    def send_halo(steps, source_of, ref, kind):
        target, cell, landing = routes[steps]
        pltpu.make_async_remote_copy(
            src_ref=source_of(cell),
            dst_ref=ref.at[landing],
            send_sem=send_sems.at[kind],
            recv_sem=recv_sems.at[kind],
            device_id=target,
            device_id_type=MESH,
        ).start()

    def all_bytes(ref, sem, number):
        part = ref.at[pl.ds(0, number)]
        return pltpu.make_async_copy(part, part, sem)

    for steps in steps_all:
        send_halo(steps, lambda cell: card_ref.at[mine], card_ref, 0)
    if far:
        to_others(send_peak, False)
    for steps in steps_all:
        send_halo(steps, lambda cell: arrived_ref.at[mine], arrived_ref, 1)

    all_bytes(card_ref, recv_sems.at[0], cells - 1).wait()
    if far:
        all_bytes(peak_ref, recv_sems.at[3], far).wait()
    highest = jnp.maximum(
        jnp.max(peak_ref[...], axis=0), jnp.max(card_ref[:, pl.ds(0, 1), :], axis=0)
    )
    fastest = jnp.max(highest, axis=1, keepdims=True)
    timestep = jnp.broadcast_to(courant / (fastest + 1e-06), (blocks, particles))
    step_ref[...] = timestep
    stores = [
        pltpu.make_async_copy(source, target, store_sems.at[number])
        for number, (source, target) in enumerate(
            ((step_ref, step_out), (half_ref, half_out), (ext_ref, ext_out))
        )
    ]
    stores[0].start()

    name = myself.astype(jnp.float32)
    slot = lax.broadcasted_iota(jnp.int32, (blocks, particles), 0).astype(jnp.float32)
    count = jnp.zeros((1, particles), jnp.float32)
    own_start = jnp.zeros((1, particles), jnp.float32)
    goals = []
    list_ref[...] = jnp.zeros_like(list_ref)
    for cell in range(cells):
        list_ref[pl.ds(cell, 1), :] = card_ref[cell, pl.ds(GHOST_ROW, 1), :]
        own = jnp.where(mine == cell, 1.0, 0.0)
        own_start = own_start + own * count
        count = count + own * (blocks - MOVERS)
        for order in range(MOVERS):
            hit = card_ref[cell, pl.ds(OWNER_ROW + order, 1), :] == name
            goals.append(jnp.where(hit, count, -1.0))
            count = count + jnp.where(hit, 1.0, 0.0)

    ids = list_ref[...]
    owners = jnp.floor((ids + 0.5) * (1.0 / blocks))
    wanted = owners == name
    lane_from = lax.broadcasted_iota(jnp.int32, (particles, particles), 0)
    lane_to = lax.broadcasted_iota(jnp.int32, (particles, particles), 1)
    earlier = jnp.where(lane_from < lane_to, 1.0, 0.0)
    ranked = jnp.dot(
        jnp.where(wanted, 1.0, 0.0), earlier, preferred_element_type=jnp.float32
    )
    for request in range(REQUESTS):
        fits = jnp.logical_and(wanted, jnp.abs(ranked - request) < 0.5)
        slots = jnp.sum(jnp.where(fits, ids - owners * blocks, 0.0), axis=1, keepdims=True)
        ask_ref[request] = jnp.broadcast_to(slots, ids.shape)

    all_bytes(arrived_ref, recv_sems.at[1], cells - 1).wait()
    settled = [jnp.zeros((blocks, particles), jnp.float32) for _ in range(STATE)]
    for cell in range(cells):
        for order in range(MOVERS):
            chosen = slot == goals[cell * MOVERS + order]
            for comp in range(STATE):
                row = arrived_ref[cell, pl.ds(order * STATE + comp, 1), :]
                settled[comp] = jnp.where(chosen, row, settled[comp])
    stayed = jnp.int32(0)
    for block in range(blocks):
        stays = jnp.where(owner_ref[block] == myself, 1, 0)
        offset = jnp.where(stays == 1, stayed, -2 * blocks * MOVERS * cells).astype(jnp.float32)
        chosen = slot == own_start + offset
        for part, source in enumerate(sources):
            for dim in range(dims):
                comp = part * dims + dim
                row = source[dim, pl.ds(block, 1), :]
                settled[comp] = jnp.where(chosen, row, settled[comp])
        stayed += stays

    for dim in range(dims):
        halfway = settled[2 * dims + dim] + 0.5 * timestep * settled[3 * dims + dim]
        half_ref[dim] = halfway
        flat_ref[pl.ds(dim * blocks, blocks), :] = settled[dim]
        flat_ref[pl.ds((dims + dim) * blocks, blocks), :] = settled[dims + dim] + timestep * halfway
    comps = 2 * dims
    blocks_rows = []
    for block in range(blocks):
        rows = flat_ref[pl.ds(block, comps, stride=blocks), :]
        ext_ref[block] = jnp.zeros((SUBLANES, particles), jnp.float32)
        ext_ref[block, pl.ds(0, comps), :] = rows
        blocks_rows.append(rows)
    for cell in range(cells):
        for request in range(REQUESTS):
            ask = jnp.broadcast_to(ask_ref[request, pl.ds(cell, 1), :], (comps, particles))
            picked = blocks_rows[0]
            for block in range(1, blocks):
                picked = jnp.where(ask == block, blocks_rows[block], picked)
            pack_ref[cell, request] = picked

    for steps in steps_all:
        send_halo(steps, lambda cell: pack_ref.at[cell], ghosts_ref, 2)
    stores[1].start()
    taken = []
    for ghost in range(ghosts):
        device = lax.div(ghost_ref[ghost], blocks)
        rest = lax.div(device, sizes[2])
        spots = (lax.div(rest, sizes[1]), lax.rem(rest, sizes[1]), lax.rem(device, sizes[2]))
        moves = []
        for spot, place, size in zip(spots, places, sizes):
            apart = lax.rem(spot - place + size, size)
            moves.append(jnp.where(apart == size - 1, -1, apart) if size > 2 else apart)
        repeats = jnp.int32(0)
        for _, before in taken:
            repeats += jnp.where(before == device, 1, 0)
        taken.append((cell_of(places, moves, sizes) * REQUESTS + repeats, device))
    for ghost in range(ghosts):
        ext_ref[blocks + ghost] = jnp.zeros((SUBLANES, particles), jnp.float32)
    all_bytes(ghosts_ref, recv_sems.at[2], cells - 1).wait()
    for ghost, (index, _) in enumerate(taken):
        rows = ghosts_ref[lax.div(index, REQUESTS), lax.rem(index, REQUESTS)]
        ext_ref[blocks + ghost, pl.ds(0, comps), :] = rows
    stores[2].start()
    all_bytes(card_ref, send_sems.at[0], cells - 1).wait()
    all_bytes(arrived_ref, send_sems.at[1], cells - 1).wait()
    all_bytes(ghosts_ref, send_sems.at[2], cells - 1).wait()
    if far:
        all_bytes(peak_ref, send_sems.at[3], far).wait()
    for store in stores:
        store.wait()


def exchange(sizes, new_owner, ghost_ids, ref_pos, displace, velocity, acceleration):
    dims, blocks, particles = ref_pos.shape
    cells = len(neighbour_steps(sizes)) + 1
    total = sizes[0] * sizes[1] * sizes[2]
    padded = -(-cells // SUBLANES) * SUBLANES
    ghosts = ghost_ids.shape[0]
    hbm = pl.BlockSpec(memory_space=pltpu.HBM)
    outs = (
        jax.ShapeDtypeStruct((blocks + ghosts, SUBLANES, particles), jnp.float32),
        jax.ShapeDtypeStruct((dims, blocks, particles), jnp.float32),
        jax.ShapeDtypeStruct((blocks, particles), jnp.float32),
    )
    return pl.pallas_call(
        functools.partial(exchange_kernel, sizes),
        out_shape=outs,
        in_specs=[hbm] * 6,
        out_specs=(hbm, hbm, hbm),
        scratch_shapes=[
            pltpu.SMEM(new_owner.shape, jnp.int32),
            pltpu.SMEM(ghost_ids.shape, jnp.int32),
            pltpu.VMEM(ref_pos.shape, jnp.float32),
            pltpu.VMEM(ref_pos.shape, jnp.float32),
            pltpu.VMEM(ref_pos.shape, jnp.float32),
            pltpu.VMEM(ref_pos.shape, jnp.float32),
            pltpu.VMEM((cells, MOVERS * STATE, particles), jnp.float32),
            pltpu.VMEM((cells, CARD, particles), jnp.float32),
            pltpu.VMEM((total, 1, particles), jnp.float32),
            pltpu.VMEM((cells, REQUESTS, 2 * dims, particles), jnp.float32),
            pltpu.VMEM((cells, REQUESTS, 2 * dims, particles), jnp.float32),
            pltpu.VMEM((padded, particles), jnp.float32),
            pltpu.VMEM((REQUESTS, padded, particles), jnp.float32),
            pltpu.VMEM((2 * dims * blocks, particles), jnp.float32),
            *[pltpu.VMEM(out.shape, jnp.float32) for out in outs],
            pltpu.SemaphoreType.DMA((4,)),
            pltpu.SemaphoreType.DMA((4,)),
            pltpu.SemaphoreType.DMA((6,)),
            pltpu.SemaphoreType.DMA((3,)),
        ],
        compiler_params=pltpu.CompilerParams(
            collective_id=0, has_side_effects=True, vmem_limit_bytes=64 * 1024 * 1024
        ),
    )(new_owner, ghost_ids, ref_pos, displace, velocity, acceleration)


def spread_away(ext_ref, rows_ref, turned_ref, sorted_ref, mask_ref, ones_ref, wide_ref):
    extended, comps, particles = ext_ref.shape
    used = wide_ref.shape[1]
    groups = wide_ref.shape[2]
    halves = sorted_ref.shape[0]
    stride = 4 * comps
    batch = particles // stride
    aligned = SUBLANES * WORD_BITS
    rows_ref[...] = jnp.zeros_like(rows_ref)
    for block in range(extended):
        rest = ext_ref[block]
        for term in range(3):
            part = rest.astype(jnp.bfloat16).astype(jnp.float32)
            rows_ref[pl.ds(block * stride + term * comps, comps), :] = part
            rest = rest - part
    for number in range(2 * halves):
        turned_ref[number] = rows_ref[pl.ds(number * particles, particles), :].T
    for number in range(2 * halves):
        half, column = number % halves, number // halves * particles
        for pair in range(groups // 2):
            parts = []
            for step in (2 * pair, 2 * pair + 1):
                if step < WORD_BITS:
                    parts.append(turned_ref[number, pl.ds(step, SUBLANES, stride=WORD_BITS), :])
                else:
                    start = aligned + (step - WORD_BITS) * SUBLANES
                    parts.append(turned_ref[number, pl.ds(start, SUBLANES), :])
            both = jnp.concatenate(parts, axis=0).astype(jnp.bfloat16)
            sorted_ref[half, pair, :, pl.ds(column, particles)] = both
    lane = lax.broadcasted_iota(jnp.int32, mask_ref.shape[2:], 1) % particles
    for block in range(batch):
        for comp in range(used):
            keep = jnp.logical_and(lane // stride == block, lane % comps == comp)
            mask_ref[block, comp] = jnp.where(keep, 1.0, 0.0).astype(jnp.bfloat16)
    above = lax.broadcasted_iota(jnp.int32, ones_ref.shape, 0) // particles
    beside = lax.broadcasted_iota(jnp.int32, ones_ref.shape, 1) // particles
    ones_ref[...] = jnp.where(above == beside, 1.0, 0.0).astype(jnp.bfloat16)

    def spread_half(half, carry):
        table = sorted_ref[half]
        for block in range(batch):
            kept = [
                (table * mask_ref[block, comp][None]).reshape(particles, 2 * particles)
                for comp in range(used)
            ]
            spread = jnp.dot(
                jnp.concatenate(kept, axis=0), ones_ref[...], preferred_element_type=jnp.float32
            )
            for side in range(2):
                part = spread[:, side * particles : (side + 1) * particles]
                place = (half + side * halves) * batch + block
                wide_ref[place] = part.reshape(used, groups, SUBLANES, particles)
        return carry

    lax.fori_loop(0, halves, spread_half, 0)


def tail_steps(particles):
    starts = range(SUBLANES * WORD_BITS, particles, SUBLANES)
    return [(start, start // WORD_BITS, (start + SUBLANES - 1) // WORD_BITS) for start in starts]


def tile_sum(home, away, front, back, wide_ref, bit_ref, particles):
    sublane = lax.broadcasted_iota(jnp.int32, (SUBLANES, particles), 0)
    sums = [jnp.zeros((SUBLANES, particles), jnp.float32) for _ in range(3)]
    tails = tail_steps(particles)
    for step in range(particles // SUBLANES):
        if step < WORD_BITS:
            hit = jnp.bitwise_and(front, 1 << step)
        else:
            start, low, high = tails[step - WORD_BITS]
            low, high = low - SUBLANES, high - SUBLANES
            row = jnp.broadcast_to(back[low : low + 1], (SUBLANES, particles))
            if high != low:
                upper = jnp.broadcast_to(back[high : high + 1], (SUBLANES, particles))
                row = jnp.where(sublane < (high + SUBLANES) * WORD_BITS - start, row, upper)
            hit = jnp.bitwise_and(row, bit_ref[step - WORD_BITS])
        other = [wide_ref[away, comp, step] for comp in range(6)]
        ref_gap = [other[k] - home[k] for k in range(3)]
        now_gap = [ref_gap[k] + (other[3 + k] - home[3 + k]) for k in range(3)]
        ref_sq = ref_gap[0] * ref_gap[0] + ref_gap[1] * ref_gap[1] + ref_gap[2] * ref_gap[2]
        now_sq = now_gap[0] * now_gap[0] + now_gap[1] * now_gap[1] + now_gap[2] * now_gap[2]
        scaled = jnp.where(hit != 0, lax.rsqrt(ref_sq) - lax.rsqrt(now_sq), 0.0)
        sums = [sums[k] + scaled * now_gap[k] for k in range(3)]
    return sums


def bond_kernel(
    words, pairs_in, bits_in, ext_in, half_in, step_in, count_ref,
    displace_ref, velocity_ref, accel_ref,
    pairs_ref, bits_ref, ext_ref, half_ref, step_ref, rows_ref, turned_ref, sorted_ref, mask_ref, ones_ref, wide_ref,
    total_ref, bit_ref, load_sems,
):
    _, blocks, particles = accel_ref.shape
    pairs = bits_ref.shape[0] // words
    outer = (ext_in, pairs_in, bits_in, half_in, step_in)
    inner = (ext_ref, pairs_ref, bits_ref, half_ref, step_ref)
    loads = [
        pltpu.make_async_copy(source, target, load_sems.at[number])
        for number, (source, target) in enumerate(zip(outer, inner))
    ]
    for load in loads:
        load.start()
    loads[0].wait()
    spread_away(ext_ref, rows_ref, turned_ref, sorted_ref, mask_ref, ones_ref, wide_ref)
    total_ref[...] = jnp.zeros_like(total_ref)
    sublane = lax.broadcasted_iota(jnp.int32, (SUBLANES, particles), 0)
    for number, (start, _, _) in enumerate(tail_steps(particles)):
        bit_ref[number] = jnp.left_shift(1, (sublane + start) % WORD_BITS)

    def not_own(first, rows):
        word = lax.broadcasted_iota(jnp.int32, (rows, particles), 0) + first
        lane = lax.broadcasted_iota(jnp.int32, (rows, particles), 1)
        own = jnp.where(lane // WORD_BITS == word, jnp.left_shift(1, lane % WORD_BITS), 0)
        return jnp.bitwise_not(own)

    behind = words - SUBLANES
    keep_front, keep_back = not_own(0, SUBLANES), not_own(SUBLANES, behind)
    count = count_ref[0]
    for load in loads[1:]:
        load.wait()

    def pair_sums(wish):
        slot = jnp.minimum(wish, pairs - 1)
        live = jnp.where(wish < count, -1, 0)
        home_id = pairs_ref[0, slot]
        away_id = pairs_ref[1, slot]
        home = [
            jnp.broadcast_to(ext_ref[home_id, pl.ds(comp, 1), :], (SUBLANES, particles))
            for comp in range(6)
        ]
        apart = jnp.where(home_id == away_id, 0, -1)
        front = bits_ref[pl.ds(slot, SUBLANES, stride=pairs), :]
        back = bits_ref[pl.ds(slot + SUBLANES * pairs, behind, stride=pairs), :]
        front = front & ((keep_front | apart) & live)
        back = back & ((keep_back | apart) & live)
        return home_id, tile_sum(home, away_id, front, back, wide_ref, bit_ref, particles)

    def add_pairs(number, carry):
        found = [pair_sums(number * TOGETHER + order) for order in range(TOGETHER)]
        for home_id, sums in found:
            for comp in range(3):
                total_ref[home_id, comp] += sums[comp]
        return carry

    lax.fori_loop(0, (count + TOGETHER - 1) // TOGETHER, add_pairs, 0)
    accel = stiffness * jnp.sum(total_ref[...], axis=2)
    for comp in range(3):
        for block in range(blocks):
            accel_ref[comp, pl.ds(block, 1), :] = accel[block, comp : comp + 1]
            displace_ref[comp, pl.ds(block, 1), :] = ext_ref[block, pl.ds(3 + comp, 1), :]
        velocity_ref[comp] = half_ref[comp] + 0.5 * step_ref[...] * accel_ref[comp]


def bond_step(ext, half, step, pair_blocks, pair_count, bond_bits):
    blocks, particles = step.shape
    extended = ext.shape[0]
    words, pairs = bond_bits.shape[0:2]
    shape = jax.ShapeDtypeStruct((3, blocks, particles), jnp.float32)
    smem = pl.BlockSpec(memory_space=pltpu.SMEM)
    vmem = pl.BlockSpec(memory_space=pltpu.VMEM)
    hbm = pl.BlockSpec(memory_space=pltpu.HBM)
    groups = particles // SUBLANES
    batch = particles // (4 * SUBLANES)
    halves = -(-extended // (2 * batch))
    return pl.pallas_call(
        functools.partial(bond_kernel, words),
        out_shape=(shape, shape, shape),
        in_specs=[hbm, hbm, hbm, hbm, hbm, smem],
        out_specs=(vmem, vmem, vmem),
        scratch_shapes=[
            pltpu.SMEM(pair_blocks.shape, jnp.int32),
            pltpu.VMEM((words * pairs, particles), jnp.int32),
            pltpu.VMEM(ext.shape, jnp.float32),
            pltpu.VMEM(half.shape, jnp.float32),
            pltpu.VMEM(step.shape, jnp.float32),
            pltpu.VMEM((2 * halves * particles, particles), jnp.float32),
            pltpu.VMEM((2 * halves, particles, particles), jnp.float32),
            pltpu.VMEM((halves, groups // 2, 2 * SUBLANES, 2 * particles), jnp.bfloat16),
            pltpu.VMEM((batch, 6, 2 * SUBLANES, 2 * particles), jnp.bfloat16),
            pltpu.VMEM((2 * particles, 2 * particles), jnp.bfloat16),
            pltpu.VMEM((2 * halves * batch, 6, groups, SUBLANES, particles), jnp.float32),
            pltpu.VMEM((blocks, 3, SUBLANES, particles), jnp.float32),
            pltpu.VMEM((len(tail_steps(particles)), SUBLANES, particles), jnp.int32),
            pltpu.SemaphoreType.DMA((5,)),
        ],
        compiler_params=pltpu.CompilerParams(vmem_limit_bytes=64 * 1024 * 1024),
    )(pair_blocks, bond_bits.reshape(words * pairs, particles), ext, half, step, pair_count)


def per_device(
    ref_pos,
    displace,
    velocity,
    acceleration,
    new_owner,
    ghost_ids,
    pair_blocks,
    pair_count,
    bond_bits,
):
    sizes = tuple(lax.axis_size(name) for name in AXES)
    turned = [array.transpose(1, 0, 2) for array in (ref_pos, displace, velocity, acceleration)]
    ext, half, step = exchange(sizes, new_owner, ghost_ids, *turned)
    results = bond_step(ext, half, step, pair_blocks, pair_count, bond_bits.transpose(1, 0, 2))
    return tuple(array.transpose(1, 0, 2) for array in results)


def solution(mesh):
    in_specs = (
        P(("gx", "gy", "gz"), None, None),
        P(("gx", "gy", "gz"), None, None),
        P(("gx", "gy", "gz"), None, None),
        P(("gx", "gy", "gz"), None, None),
        P(("gx", "gy", "gz")),
        P(("gx", "gy", "gz")),
        P(None, ("gx", "gy", "gz")),
        P(("gx", "gy", "gz")),
        P(("gx", "gy", "gz"), None, None),
    )
    out_specs = (
        P(("gx", "gy", "gz"), None, None),
        P(("gx", "gy", "gz"), None, None),
        P(("gx", "gy", "gz"), None, None),
    )
    return jax.shard_map(
        per_device, mesh=mesh, in_specs=in_specs, out_specs=out_specs, check_vma=False
    )
```

```python
import functools

import jax
import jax.numpy as jnp
from jax import lax
from jax.experimental import pallas as pl
from jax.experimental.pallas import tpu as pltpu
from jax.sharding import PartitionSpec as P

WORD_BITS = 11


courant = 0.05
stiffness = 20.0


MESH = pl.DeviceIdType.MESH
AXES = ("gx", "gy", "gz")
MOVERS = 2
REQUESTS = 3
STATE = 12
SUBLANES = 8
OWNER_ROW = 1
GHOST_ROW = OWNER_ROW + MOVERS
CARD = GHOST_ROW + 1
UNROLLED = 64
TOGETHER = 4


def reach(size):
    return (0,) if size == 1 else (0, 1) if size == 2 else (-1, 0, 1)


def cell_rank(place, step, size):
    if size < 3:
        return (place + step) % size
    first = (size - place) // size
    last = (place + 1) // size
    return (step + 1 + 2 * first + last) % 3


def cell_of(places, steps, sizes):
    cell = 0
    for place, step, size in zip(places, steps, sizes):
        cell = cell * len(reach(size)) + cell_rank(place, step, size)
    return cell


def neighbour_steps(sizes):
    every = [(x, y, z) for x in reach(sizes[0]) for y in reach(sizes[1]) for z in reach(sizes[2])]
    return [steps for steps in every if steps != (0, 0, 0)]


def exchange_kernel(
    sizes,
    owner_in, ghost_in, ref_in, disp_in, vel_in, acc_in,
    ext_out, half_out, step_out,
    owner_ref, ghost_ref, ref_ref, disp_ref, vel_ref, acc_ref,
    arrived_ref, card_ref, peak_ref, pack_ref, ghosts_ref, list_ref, ask_ref, flat_ref,
    ext_ref, half_ref, step_ref,
    send_sems, recv_sems, load_sems, store_sems,
):
    dims, blocks, particles = ref_ref.shape
    inner = (owner_ref, ghost_ref, ref_ref, disp_ref, vel_ref, acc_ref)
    outer = (owner_in, ghost_in, ref_in, disp_in, vel_in, acc_in)
    loads = [
        pltpu.make_async_copy(source, target, load_sems.at[number])
        for number, (source, target) in enumerate(zip(outer, inner))
    ]
    for load in loads:
        load.start()
    total = sizes[0] * sizes[1] * sizes[2]
    steps_all = sorted(neighbour_steps(sizes), key=lambda steps: -abs(steps[0]))
    cells = len(steps_all) + 1
    far = total - cells if total <= UNROLLED else total - 1
    places = [lax.axis_index(name) for name in AXES]
    myself = (places[0] * sizes[1] + places[1]) * sizes[2] + places[2]
    mine = cell_of(places, (0, 0, 0), sizes)
    routes = {}
    for steps in steps_all:
        target = [(place + step) % size for place, step, size in zip(places, steps, sizes)]
        back = [-step for step in steps]
        routes[steps] = (
            tuple(target), cell_of(places, steps, sizes), cell_of(target, back, sizes)
        )
    sources = (ref_ref, disp_ref, vel_ref, acc_ref)

    def to_others(action, near):
        if total <= UNROLLED:
            coords = [
                [(place + step) % size for step in range(size)]
                for place, size in zip(places, sizes)
            ]
            for x in range(sizes[0]):
                for y in range(sizes[1]):
                    for z in range(sizes[2]):
                        wraps = zip((x, y, z), sizes)
                        beside = all(step in (0, 1, size - 1) for step, size in wraps)
                        if (x, y, z) != (0, 0, 0) and (near or not beside):
                            action((coords[0][x], coords[1][y], coords[2][z]))
        else:

            def act(number, carry):
                device = (myself + number) % total
                rest = device // sizes[2]
                action((rest // sizes[1], rest % sizes[1], device % sizes[2]))
                return carry

            lax.fori_loop(1, total, act, 0)

    peak_ref[...] = jnp.zeros_like(peak_ref)
    barrier = pltpu.get_barrier_semaphore()
    to_others(
        lambda target: pl.semaphore_signal(barrier, inc=1, device_id=target, device_id_type=MESH),
        True,
    )

    for load in loads:
        load.wait()
    leavers = [jnp.int32(0) for _ in range(MOVERS)]
    seen = jnp.int32(0)
    for block in range(blocks):
        leaves = jnp.where(owner_ref[block] != myself, 1, 0)
        for order in range(MOVERS):
            leavers[order] += block * leaves * jnp.where(seen == order, 1, 0)
        seen += leaves
    speeds = jnp.max(jnp.abs(vel_ref[...]), axis=0)
    peak = jnp.max(speeds, axis=0, keepdims=True)
    card_ref[mine, pl.ds(0, 1), :] = peak
    peak_ref[myself] = peak
    for order in range(MOVERS):
        owner = jnp.full((1, particles), owner_ref[leavers[order]], jnp.int32)
        card_ref[mine, pl.ds(OWNER_ROW + order, 1), :] = owner.astype(jnp.float32)
    ghosts = ghost_ref.shape[0]
    lane = lax.broadcasted_iota(jnp.int32, (1, particles), 1)
    wish = jnp.full((1, particles), -blocks, jnp.int32)
    for ghost in range(ghosts):
        wish = jnp.where(lane == ghost, ghost_ref[ghost], wish)
    card_ref[mine, pl.ds(GHOST_ROW, 1), :] = wish.astype(jnp.float32)
    for order in range(MOVERS):
        for part, source in enumerate(sources):
            for dim in range(dims):
                row = order * STATE + part * dims + dim
                arrived_ref[mine, pl.ds(row, 1), :] = source[dim, pl.ds(leavers[order], 1), :]

    pl.semaphore_wait(barrier, total - 1)

    def send_peak(target):
        pltpu.make_async_remote_copy(
            src_ref=peak_ref.at[myself],
            dst_ref=peak_ref.at[myself],
            send_sem=send_sems.at[3],
            recv_sem=recv_sems.at[3],
            device_id=target,
            device_id_type=MESH,
        ).start()

    def send_halo(steps, source_of, ref, kind):
        target, cell, landing = routes[steps]
        pltpu.make_async_remote_copy(
            src_ref=source_of(cell),
            dst_ref=ref.at[landing],
            send_sem=send_sems.at[kind],
            recv_sem=recv_sems.at[kind],
            device_id=target,
            device_id_type=MESH,
        ).start()

    def all_bytes(ref, sem, number):
        part = ref.at[pl.ds(0, number)]
        return pltpu.make_async_copy(part, part, sem)

    for steps in steps_all:
        send_halo(steps, lambda cell: card_ref.at[mine], card_ref, 0)
    if far:
        to_others(send_peak, False)
    for steps in steps_all:
        send_halo(steps, lambda cell: arrived_ref.at[mine], arrived_ref, 1)

    all_bytes(card_ref, recv_sems.at[0], cells - 1).wait()
    if far:
        all_bytes(peak_ref, recv_sems.at[3], far).wait()
    highest = jnp.maximum(
        jnp.max(peak_ref[...], axis=0), jnp.max(card_ref[:, pl.ds(0, 1), :], axis=0)
    )
    fastest = jnp.max(highest, axis=1, keepdims=True)
    timestep = jnp.broadcast_to(courant / (fastest + 1e-06), (blocks, particles))
    step_ref[...] = timestep
    stores = [
        pltpu.make_async_copy(source, target, store_sems.at[number])
        for number, (source, target) in enumerate(
            ((step_ref, step_out), (half_ref, half_out), (ext_ref, ext_out))
        )
    ]
    stores[0].start()

    name = myself.astype(jnp.float32)
    slot = lax.broadcasted_iota(jnp.int32, (blocks, particles), 0).astype(jnp.float32)
    count = jnp.zeros((1, particles), jnp.float32)
    own_start = jnp.zeros((1, particles), jnp.float32)
    goals = []
    list_ref[...] = jnp.zeros_like(list_ref)
    for cell in range(cells):
        list_ref[pl.ds(cell, 1), :] = card_ref[cell, pl.ds(GHOST_ROW, 1), :]
        own = jnp.where(mine == cell, 1.0, 0.0)
        own_start = own_start + own * count
        count = count + own * (blocks - MOVERS)
        for order in range(MOVERS):
            hit = card_ref[cell, pl.ds(OWNER_ROW + order, 1), :] == name
            goals.append(jnp.where(hit, count, -1.0))
            count = count + jnp.where(hit, 1.0, 0.0)

    ids = list_ref[...]
    owners = jnp.floor((ids + 0.5) * (1.0 / blocks))
    wanted = owners == name
    lane_from = lax.broadcasted_iota(jnp.int32, (particles, particles), 0)
    lane_to = lax.broadcasted_iota(jnp.int32, (particles, particles), 1)
    earlier = jnp.where(lane_from < lane_to, 1.0, 0.0)
    ranked = jnp.dot(
        jnp.where(wanted, 1.0, 0.0), earlier, preferred_element_type=jnp.float32
    )
    for request in range(REQUESTS):
        fits = jnp.logical_and(wanted, jnp.abs(ranked - request) < 0.5)
        slots = jnp.sum(jnp.where(fits, ids - owners * blocks, 0.0), axis=1, keepdims=True)
        ask_ref[request] = jnp.broadcast_to(slots, ids.shape)

    all_bytes(arrived_ref, recv_sems.at[1], cells - 1).wait()
    settled = [jnp.zeros((blocks, particles), jnp.float32) for _ in range(STATE)]
    for cell in range(cells):
        for order in range(MOVERS):
            chosen = slot == goals[cell * MOVERS + order]
            for comp in range(STATE):
                row = arrived_ref[cell, pl.ds(order * STATE + comp, 1), :]
                settled[comp] = jnp.where(chosen, row, settled[comp])
    stayed = jnp.int32(0)
    for block in range(blocks):
        stays = jnp.where(owner_ref[block] == myself, 1, 0)
        offset = jnp.where(stays == 1, stayed, -2 * blocks * MOVERS * cells).astype(jnp.float32)
        chosen = slot == own_start + offset
        for part, source in enumerate(sources):
            for dim in range(dims):
                comp = part * dims + dim
                row = source[dim, pl.ds(block, 1), :]
                settled[comp] = jnp.where(chosen, row, settled[comp])
        stayed += stays

    for dim in range(dims):
        halfway = settled[2 * dims + dim] + 0.5 * timestep * settled[3 * dims + dim]
        half_ref[dim] = halfway
        flat_ref[pl.ds(dim * blocks, blocks), :] = settled[dim]
        flat_ref[pl.ds((dims + dim) * blocks, blocks), :] = settled[dims + dim] + timestep * halfway
    comps = 2 * dims
    blocks_rows = []
    for block in range(blocks):
        rows = flat_ref[pl.ds(block, comps, stride=blocks), :]
        ext_ref[block] = jnp.zeros((SUBLANES, particles), jnp.float32)
        ext_ref[block, pl.ds(0, comps), :] = rows
        blocks_rows.append(rows)
    for cell in range(cells):
        for request in range(REQUESTS):
            ask = jnp.broadcast_to(ask_ref[request, pl.ds(cell, 1), :], (comps, particles))
            picked = blocks_rows[0]
            for block in range(1, blocks):
                picked = jnp.where(ask == block, blocks_rows[block], picked)
            pack_ref[cell, request] = picked

    for steps in steps_all:
        send_halo(steps, lambda cell: pack_ref.at[cell], ghosts_ref, 2)
    stores[1].start()
    taken = []
    for ghost in range(ghosts):
        device = lax.div(ghost_ref[ghost], blocks)
        rest = lax.div(device, sizes[2])
        spots = (lax.div(rest, sizes[1]), lax.rem(rest, sizes[1]), lax.rem(device, sizes[2]))
        moves = []
        for spot, place, size in zip(spots, places, sizes):
            apart = lax.rem(spot - place + size, size)
            moves.append(jnp.where(apart == size - 1, -1, apart) if size > 2 else apart)
        repeats = jnp.int32(0)
        for _, before in taken:
            repeats += jnp.where(before == device, 1, 0)
        taken.append((cell_of(places, moves, sizes) * REQUESTS + repeats, device))
    for ghost in range(ghosts):
        ext_ref[blocks + ghost] = jnp.zeros((SUBLANES, particles), jnp.float32)
    all_bytes(ghosts_ref, recv_sems.at[2], cells - 1).wait()
    for ghost, (index, _) in enumerate(taken):
        rows = ghosts_ref[lax.div(index, REQUESTS), lax.rem(index, REQUESTS)]
        ext_ref[blocks + ghost, pl.ds(0, comps), :] = rows
    stores[2].start()
    all_bytes(card_ref, send_sems.at[0], cells - 1).wait()
    all_bytes(arrived_ref, send_sems.at[1], cells - 1).wait()
    all_bytes(ghosts_ref, send_sems.at[2], cells - 1).wait()
    if far:
        all_bytes(peak_ref, send_sems.at[3], far).wait()
    for store in stores:
        store.wait()


def exchange(sizes, new_owner, ghost_ids, ref_pos, displace, velocity, acceleration):
    dims, blocks, particles = ref_pos.shape
    cells = len(neighbour_steps(sizes)) + 1
    total = sizes[0] * sizes[1] * sizes[2]
    padded = -(-cells // SUBLANES) * SUBLANES
    ghosts = ghost_ids.shape[0]
    hbm = pl.BlockSpec(memory_space=pltpu.HBM)
    outs = (
        jax.ShapeDtypeStruct((blocks + ghosts, SUBLANES, particles), jnp.float32),
        jax.ShapeDtypeStruct((dims, blocks, particles), jnp.float32),
        jax.ShapeDtypeStruct((blocks, particles), jnp.float32),
    )
    return pl.pallas_call(
        functools.partial(exchange_kernel, sizes),
        out_shape=outs,
        in_specs=[hbm] * 6,
        out_specs=(hbm, hbm, hbm),
        scratch_shapes=[
            pltpu.SMEM(new_owner.shape, jnp.int32),
            pltpu.SMEM(ghost_ids.shape, jnp.int32),
            pltpu.VMEM(ref_pos.shape, jnp.float32),
            pltpu.VMEM(ref_pos.shape, jnp.float32),
            pltpu.VMEM(ref_pos.shape, jnp.float32),
            pltpu.VMEM(ref_pos.shape, jnp.float32),
            pltpu.VMEM((cells, MOVERS * STATE, particles), jnp.float32),
            pltpu.VMEM((cells, CARD, particles), jnp.float32),
            pltpu.VMEM((total, 1, particles), jnp.float32),
            pltpu.VMEM((cells, REQUESTS, 2 * dims, particles), jnp.float32),
            pltpu.VMEM((cells, REQUESTS, 2 * dims, particles), jnp.float32),
            pltpu.VMEM((padded, particles), jnp.float32),
            pltpu.VMEM((REQUESTS, padded, particles), jnp.float32),
            pltpu.VMEM((2 * dims * blocks, particles), jnp.float32),
            *[pltpu.VMEM(out.shape, jnp.float32) for out in outs],
            pltpu.SemaphoreType.DMA((4,)),
            pltpu.SemaphoreType.DMA((4,)),
            pltpu.SemaphoreType.DMA((6,)),
            pltpu.SemaphoreType.DMA((3,)),
        ],
        compiler_params=pltpu.CompilerParams(
            collective_id=0, has_side_effects=True, vmem_limit_bytes=64 * 1024 * 1024
        ),
    )(new_owner, ghost_ids, ref_pos, displace, velocity, acceleration)


def spread_away(ready, ext_ref, rows_ref, turned_ref, sorted_ref, mask_ref, ones_ref, wide_ref):
    extended, comps, particles = ext_ref.shape
    used = wide_ref.shape[1]
    groups = wide_ref.shape[2]
    halves = sorted_ref.shape[0]
    stride = 4 * comps
    batch = particles // stride
    aligned = SUBLANES * WORD_BITS
    rows_ref[...] = jnp.zeros_like(rows_ref)
    lane = lax.broadcasted_iota(jnp.int32, mask_ref.shape[2:], 1) % particles
    for block in range(batch):
        for comp in range(used):
            keep = jnp.logical_and(lane // stride == block, lane % comps == comp)
            mask_ref[block, comp] = jnp.where(keep, 1.0, 0.0).astype(jnp.bfloat16)
    above = lax.broadcasted_iota(jnp.int32, ones_ref.shape, 0) // particles
    beside = lax.broadcasted_iota(jnp.int32, ones_ref.shape, 1) // particles
    ones_ref[...] = jnp.where(above == beside, 1.0, 0.0).astype(jnp.bfloat16)
    ready()
    for block in range(extended):
        rest = ext_ref[block]
        for term in range(3):
            part = rest.astype(jnp.bfloat16).astype(jnp.float32)
            rows_ref[pl.ds(block * stride + term * comps, comps), :] = part
            rest = rest - part
    for number in range(2 * halves):
        turned_ref[number] = rows_ref[pl.ds(number * particles, particles), :].T
    for number in range(2 * halves):
        half, column = number % halves, number // halves * particles
        for pair in range(groups // 2):
            parts = []
            for step in (2 * pair, 2 * pair + 1):
                if step < WORD_BITS:
                    parts.append(turned_ref[number, pl.ds(step, SUBLANES, stride=WORD_BITS), :])
                else:
                    start = aligned + (step - WORD_BITS) * SUBLANES
                    parts.append(turned_ref[number, pl.ds(start, SUBLANES), :])
            both = jnp.concatenate(parts, axis=0).astype(jnp.bfloat16)
            sorted_ref[half, pair, :, pl.ds(column, particles)] = both
    def spread_half(half, carry):
        table = sorted_ref[half]
        for block in range(batch):
            kept = [
                (table * mask_ref[block, comp][None]).reshape(particles, 2 * particles)
                for comp in range(used)
            ]
            spread = jnp.dot(
                jnp.concatenate(kept, axis=0), ones_ref[...], preferred_element_type=jnp.float32
            )
            for side in range(2):
                part = spread[:, side * particles : (side + 1) * particles]
                place = (half + side * halves) * batch + block
                wide_ref[place] = part.reshape(used, groups, SUBLANES, particles)
        return carry

    lax.fori_loop(0, halves, spread_half, 0)


def tail_steps(particles):
    starts = range(SUBLANES * WORD_BITS, particles, SUBLANES)
    return [(start, start // WORD_BITS, (start + SUBLANES - 1) // WORD_BITS) for start in starts]


def tile_sum(home, away, front, back, wide_ref, bit_ref, particles):
    sublane = lax.broadcasted_iota(jnp.int32, (SUBLANES, particles), 0)
    sums = [jnp.zeros((SUBLANES, particles), jnp.float32) for _ in range(3)]
    tails = tail_steps(particles)
    for step in range(particles // SUBLANES):
        if step < WORD_BITS:
            hit = jnp.bitwise_and(front, 1 << step)
        else:
            start, low, high = tails[step - WORD_BITS]
            low, high = low - SUBLANES, high - SUBLANES
            row = jnp.broadcast_to(back[low : low + 1], (SUBLANES, particles))
            if high != low:
                upper = jnp.broadcast_to(back[high : high + 1], (SUBLANES, particles))
                row = jnp.where(sublane < (high + SUBLANES) * WORD_BITS - start, row, upper)
            hit = jnp.bitwise_and(row, bit_ref[step - WORD_BITS])
        other = [wide_ref[away, comp, step] for comp in range(6)]
        ref_gap = [other[k] - home[k] for k in range(3)]
        now_gap = [ref_gap[k] + (other[3 + k] - home[3 + k]) for k in range(3)]
        ref_sq = ref_gap[0] * ref_gap[0] + ref_gap[1] * ref_gap[1] + ref_gap[2] * ref_gap[2]
        now_sq = now_gap[0] * now_gap[0] + now_gap[1] * now_gap[1] + now_gap[2] * now_gap[2]
        scaled = jnp.where(hit != 0, lax.rsqrt(ref_sq) - lax.rsqrt(now_sq), 0.0)
        sums = [sums[k] + scaled * now_gap[k] for k in range(3)]
    return sums


def bond_kernel(
    words, pairs_in, bits_in, ext_in, half_in, step_in, count_ref,
    displace_ref, velocity_ref, accel_ref,
    pairs_ref, bits_ref, ext_ref, half_ref, step_ref, rows_ref, turned_ref, sorted_ref, mask_ref, ones_ref, wide_ref,
    total_ref, bit_ref, load_sems,
):
    _, blocks, particles = accel_ref.shape
    pairs = bits_ref.shape[0] // words
    outer = (ext_in, pairs_in, bits_in, half_in, step_in)
    inner = (ext_ref, pairs_ref, bits_ref, half_ref, step_ref)
    loads = [
        pltpu.make_async_copy(source, target, load_sems.at[number])
        for number, (source, target) in enumerate(zip(outer, inner))
    ]
    for load in loads:
        load.start()
    total_ref[...] = jnp.zeros_like(total_ref)
    sublane = lax.broadcasted_iota(jnp.int32, (SUBLANES, particles), 0)
    for number, (start, _, _) in enumerate(tail_steps(particles)):
        bit_ref[number] = jnp.left_shift(1, (sublane + start) % WORD_BITS)

    spread_away(
        loads[0].wait, ext_ref, rows_ref, turned_ref, sorted_ref, mask_ref, ones_ref, wide_ref
    )

    def not_own(first, rows):
        word = lax.broadcasted_iota(jnp.int32, (rows, particles), 0) + first
        lane = lax.broadcasted_iota(jnp.int32, (rows, particles), 1)
        own = jnp.where(lane // WORD_BITS == word, jnp.left_shift(1, lane % WORD_BITS), 0)
        return jnp.bitwise_not(own)

    behind = words - SUBLANES
    keep_front, keep_back = not_own(0, SUBLANES), not_own(SUBLANES, behind)
    count = count_ref[0]
    for load in loads[1:]:
        load.wait()

    def pair_sums(wish):
        slot = jnp.minimum(wish, pairs - 1)
        live = jnp.where(wish < count, -1, 0)
        home_id = pairs_ref[0, slot]
        away_id = pairs_ref[1, slot]
        home = [
            jnp.broadcast_to(ext_ref[home_id, pl.ds(comp, 1), :], (SUBLANES, particles))
            for comp in range(6)
        ]
        apart = jnp.where(home_id == away_id, 0, -1)
        front = bits_ref[pl.ds(slot, SUBLANES, stride=pairs), :]
        back = bits_ref[pl.ds(slot + SUBLANES * pairs, behind, stride=pairs), :]
        front = front & ((keep_front | apart) & live)
        back = back & ((keep_back | apart) & live)
        return home_id, tile_sum(home, away_id, front, back, wide_ref, bit_ref, particles)

    def add_pairs(number, carry):
        found = [pair_sums(number * TOGETHER + order) for order in range(TOGETHER)]
        for home_id, sums in found:
            for comp in range(3):
                total_ref[home_id, comp] += sums[comp]
        return carry

    lax.fori_loop(0, (count + TOGETHER - 1) // TOGETHER, add_pairs, 0)
    accel = stiffness * jnp.sum(total_ref[...], axis=2)
    for comp in range(3):
        for block in range(blocks):
            accel_ref[comp, pl.ds(block, 1), :] = accel[block, comp : comp + 1]
            displace_ref[comp, pl.ds(block, 1), :] = ext_ref[block, pl.ds(3 + comp, 1), :]
        velocity_ref[comp] = half_ref[comp] + 0.5 * step_ref[...] * accel_ref[comp]


def bond_step(ext, half, step, pair_blocks, pair_count, bond_bits):
    blocks, particles = step.shape
    extended = ext.shape[0]
    words, pairs = bond_bits.shape[0:2]
    shape = jax.ShapeDtypeStruct((3, blocks, particles), jnp.float32)
    smem = pl.BlockSpec(memory_space=pltpu.SMEM)
    vmem = pl.BlockSpec(memory_space=pltpu.VMEM)
    hbm = pl.BlockSpec(memory_space=pltpu.HBM)
    groups = particles // SUBLANES
    batch = particles // (4 * SUBLANES)
    halves = -(-extended // (2 * batch))
    return pl.pallas_call(
        functools.partial(bond_kernel, words),
        out_shape=(shape, shape, shape),
        in_specs=[hbm, hbm, hbm, hbm, hbm, smem],
        out_specs=(vmem, vmem, vmem),
        scratch_shapes=[
            pltpu.SMEM(pair_blocks.shape, jnp.int32),
            pltpu.VMEM((words * pairs, particles), jnp.int32),
            pltpu.VMEM(ext.shape, jnp.float32),
            pltpu.VMEM(half.shape, jnp.float32),
            pltpu.VMEM(step.shape, jnp.float32),
            pltpu.VMEM((2 * halves * particles, particles), jnp.float32),
            pltpu.VMEM((2 * halves, particles, particles), jnp.float32),
            pltpu.VMEM((halves, groups // 2, 2 * SUBLANES, 2 * particles), jnp.bfloat16),
            pltpu.VMEM((batch, 6, 2 * SUBLANES, 2 * particles), jnp.bfloat16),
            pltpu.VMEM((2 * particles, 2 * particles), jnp.bfloat16),
            pltpu.VMEM((2 * halves * batch, 6, groups, SUBLANES, particles), jnp.float32),
            pltpu.VMEM((blocks, 3, SUBLANES, particles), jnp.float32),
            pltpu.VMEM((len(tail_steps(particles)), SUBLANES, particles), jnp.int32),
            pltpu.SemaphoreType.DMA((5,)),
        ],
        compiler_params=pltpu.CompilerParams(vmem_limit_bytes=64 * 1024 * 1024),
    )(pair_blocks, bond_bits.reshape(words * pairs, particles), ext, half, step, pair_count)


def per_device(
    ref_pos,
    displace,
    velocity,
    acceleration,
    new_owner,
    ghost_ids,
    pair_blocks,
    pair_count,
    bond_bits,
):
    sizes = tuple(lax.axis_size(name) for name in AXES)
    turned = [array.transpose(1, 0, 2) for array in (ref_pos, displace, velocity, acceleration)]
    ext, half, step = exchange(sizes, new_owner, ghost_ids, *turned)
    results = bond_step(ext, half, step, pair_blocks, pair_count, bond_bits.transpose(1, 0, 2))
    return tuple(array.transpose(1, 0, 2) for array in results)


def solution(mesh):
    in_specs = (
        P(("gx", "gy", "gz"), None, None),
        P(("gx", "gy", "gz"), None, None),
        P(("gx", "gy", "gz"), None, None),
        P(("gx", "gy", "gz"), None, None),
        P(("gx", "gy", "gz")),
        P(("gx", "gy", "gz")),
        P(None, ("gx", "gy", "gz")),
        P(("gx", "gy", "gz")),
        P(("gx", "gy", "gz"), None, None),
    )
    out_specs = (
        P(("gx", "gy", "gz"), None, None),
        P(("gx", "gy", "gz"), None, None),
        P(("gx", "gy", "gz"), None, None),
    )
    return jax.shard_map(
        per_device, mesh=mesh, in_specs=in_specs, out_specs=out_specs, check_vma=False
    )
```

```python
import functools

import jax
import jax.numpy as jnp
from jax import lax
from jax.experimental import pallas as pl
from jax.experimental.pallas import tpu as pltpu
from jax.sharding import PartitionSpec as P

WORD_BITS = 11


courant = 0.05
stiffness = 20.0


MESH = pl.DeviceIdType.MESH
AXES = ("gx", "gy", "gz")
MOVERS = 2
REQUESTS = 3
STATE = 12
SUBLANES = 8
OWNER_ROW = 1
GHOST_ROW = OWNER_ROW + MOVERS
CARD = GHOST_ROW + 1
UNROLLED = 64
TOGETHER = 8


def reach(size):
    return (0,) if size == 1 else (0, 1) if size == 2 else (-1, 0, 1)


def cell_rank(place, step, size):
    if size < 3:
        return (place + step) % size
    first = (size - place) // size
    last = (place + 1) // size
    return (step + 1 + 2 * first + last) % 3


def cell_of(places, steps, sizes):
    cell = 0
    for place, step, size in zip(places, steps, sizes):
        cell = cell * len(reach(size)) + cell_rank(place, step, size)
    return cell


def neighbour_steps(sizes):
    every = [(x, y, z) for x in reach(sizes[0]) for y in reach(sizes[1]) for z in reach(sizes[2])]
    return [steps for steps in every if steps != (0, 0, 0)]


def exchange_kernel(
    sizes,
    owner_in, ghost_in, ref_in, disp_in, vel_in, acc_in,
    ext_out, half_out, step_out,
    owner_ref, ghost_ref, ref_ref, disp_ref, vel_ref, acc_ref,
    arrived_ref, card_ref, peak_ref, pack_ref, ghosts_ref, list_ref, ask_ref, flat_ref,
    ext_ref, half_ref, step_ref,
    send_sems, recv_sems, load_sems, store_sems,
):
    dims, blocks, particles = ref_ref.shape
    inner = (owner_ref, ghost_ref, ref_ref, disp_ref, vel_ref, acc_ref)
    outer = (owner_in, ghost_in, ref_in, disp_in, vel_in, acc_in)
    loads = [
        pltpu.make_async_copy(source, target, load_sems.at[number])
        for number, (source, target) in enumerate(zip(outer, inner))
    ]
    for load in loads:
        load.start()
    total = sizes[0] * sizes[1] * sizes[2]
    steps_all = sorted(neighbour_steps(sizes), key=lambda steps: -abs(steps[0]))
    cells = len(steps_all) + 1
    far = total - cells if total <= UNROLLED else total - 1
    places = [lax.axis_index(name) for name in AXES]
    myself = (places[0] * sizes[1] + places[1]) * sizes[2] + places[2]
    mine = cell_of(places, (0, 0, 0), sizes)
    routes = {}
    for steps in steps_all:
        target = [(place + step) % size for place, step, size in zip(places, steps, sizes)]
        back = [-step for step in steps]
        routes[steps] = (
            tuple(target), cell_of(places, steps, sizes), cell_of(target, back, sizes)
        )
    sources = (ref_ref, disp_ref, vel_ref, acc_ref)

    def to_others(action, near):
        if total <= UNROLLED:
            coords = [
                [(place + step) % size for step in range(size)]
                for place, size in zip(places, sizes)
            ]
            for x in range(sizes[0]):
                for y in range(sizes[1]):
                    for z in range(sizes[2]):
                        wraps = zip((x, y, z), sizes)
                        beside = all(step in (0, 1, size - 1) for step, size in wraps)
                        if (x, y, z) != (0, 0, 0) and (near or not beside):
                            action((coords[0][x], coords[1][y], coords[2][z]))
        else:

            def act(number, carry):
                device = (myself + number) % total
                rest = device // sizes[2]
                action((rest // sizes[1], rest % sizes[1], device % sizes[2]))
                return carry

            lax.fori_loop(1, total, act, 0)

    peak_ref[...] = jnp.zeros_like(peak_ref)
    barrier = pltpu.get_barrier_semaphore()
    to_others(
        lambda target: pl.semaphore_signal(barrier, inc=1, device_id=target, device_id_type=MESH),
        True,
    )

    for load in loads:
        load.wait()
    leavers = [jnp.int32(0) for _ in range(MOVERS)]
    seen = jnp.int32(0)
    for block in range(blocks):
        leaves = jnp.where(owner_ref[block] != myself, 1, 0)
        for order in range(MOVERS):
            leavers[order] += block * leaves * jnp.where(seen == order, 1, 0)
        seen += leaves
    speeds = jnp.max(jnp.abs(vel_ref[...]), axis=0)
    peak = jnp.max(speeds, axis=0, keepdims=True)
    card_ref[mine, pl.ds(0, 1), :] = peak
    peak_ref[myself] = peak
    for order in range(MOVERS):
        owner = jnp.full((1, particles), owner_ref[leavers[order]], jnp.int32)
        card_ref[mine, pl.ds(OWNER_ROW + order, 1), :] = owner.astype(jnp.float32)
    ghosts = ghost_ref.shape[0]
    lane = lax.broadcasted_iota(jnp.int32, (1, particles), 1)
    wish = jnp.full((1, particles), -blocks, jnp.int32)
    for ghost in range(ghosts):
        wish = jnp.where(lane == ghost, ghost_ref[ghost], wish)
    card_ref[mine, pl.ds(GHOST_ROW, 1), :] = wish.astype(jnp.float32)
    for order in range(MOVERS):
        for part, source in enumerate(sources):
            for dim in range(dims):
                row = order * STATE + part * dims + dim
                arrived_ref[mine, pl.ds(row, 1), :] = source[dim, pl.ds(leavers[order], 1), :]

    pl.semaphore_wait(barrier, total - 1)

    def send_peak(target):
        pltpu.make_async_remote_copy(
            src_ref=peak_ref.at[myself],
            dst_ref=peak_ref.at[myself],
            send_sem=send_sems.at[3],
            recv_sem=recv_sems.at[3],
            device_id=target,
            device_id_type=MESH,
        ).start()

    def send_halo(steps, source_of, ref, kind):
        target, cell, landing = routes[steps]
        pltpu.make_async_remote_copy(
            src_ref=source_of(cell),
            dst_ref=ref.at[landing],
            send_sem=send_sems.at[kind],
            recv_sem=recv_sems.at[kind],
            device_id=target,
            device_id_type=MESH,
        ).start()

    def all_bytes(ref, sem, number):
        part = ref.at[pl.ds(0, number)]
        return pltpu.make_async_copy(part, part, sem)

    for steps in steps_all:
        send_halo(steps, lambda cell: card_ref.at[mine], card_ref, 0)
    if far:
        to_others(send_peak, False)
    for steps in steps_all:
        send_halo(steps, lambda cell: arrived_ref.at[mine], arrived_ref, 1)

    all_bytes(card_ref, recv_sems.at[0], cells - 1).wait()
    if far:
        all_bytes(peak_ref, recv_sems.at[3], far).wait()
    highest = jnp.maximum(
        jnp.max(peak_ref[...], axis=0), jnp.max(card_ref[:, pl.ds(0, 1), :], axis=0)
    )
    fastest = jnp.max(highest, axis=1, keepdims=True)
    timestep = jnp.broadcast_to(courant / (fastest + 1e-06), (blocks, particles))
    step_ref[...] = timestep
    stores = [
        pltpu.make_async_copy(source, target, store_sems.at[number])
        for number, (source, target) in enumerate(
            ((step_ref, step_out), (half_ref, half_out), (ext_ref, ext_out))
        )
    ]
    stores[0].start()

    name = myself.astype(jnp.float32)
    slot = lax.broadcasted_iota(jnp.int32, (blocks, particles), 0).astype(jnp.float32)
    count = jnp.zeros((1, particles), jnp.float32)
    own_start = jnp.zeros((1, particles), jnp.float32)
    goals = []
    list_ref[...] = jnp.zeros_like(list_ref)
    for cell in range(cells):
        list_ref[pl.ds(cell, 1), :] = card_ref[cell, pl.ds(GHOST_ROW, 1), :]
        own = jnp.where(mine == cell, 1.0, 0.0)
        own_start = own_start + own * count
        count = count + own * (blocks - MOVERS)
        for order in range(MOVERS):
            hit = card_ref[cell, pl.ds(OWNER_ROW + order, 1), :] == name
            goals.append(jnp.where(hit, count, -1.0))
            count = count + jnp.where(hit, 1.0, 0.0)

    ids = list_ref[...]
    owners = jnp.floor((ids + 0.5) * (1.0 / blocks))
    wanted = owners == name
    lane_from = lax.broadcasted_iota(jnp.int32, (particles, particles), 0)
    lane_to = lax.broadcasted_iota(jnp.int32, (particles, particles), 1)
    earlier = jnp.where(lane_from < lane_to, 1.0, 0.0)
    ranked = jnp.dot(
        jnp.where(wanted, 1.0, 0.0), earlier, preferred_element_type=jnp.float32
    )
    for request in range(REQUESTS):
        fits = jnp.logical_and(wanted, jnp.abs(ranked - request) < 0.5)
        slots = jnp.sum(jnp.where(fits, ids - owners * blocks, 0.0), axis=1, keepdims=True)
        ask_ref[request] = jnp.broadcast_to(slots, ids.shape)

    all_bytes(arrived_ref, recv_sems.at[1], cells - 1).wait()
    settled = [jnp.zeros((blocks, particles), jnp.float32) for _ in range(STATE)]
    for cell in range(cells):
        for order in range(MOVERS):
            chosen = slot == goals[cell * MOVERS + order]
            for comp in range(STATE):
                row = arrived_ref[cell, pl.ds(order * STATE + comp, 1), :]
                settled[comp] = jnp.where(chosen, row, settled[comp])
    stayed = jnp.int32(0)
    for block in range(blocks):
        stays = jnp.where(owner_ref[block] == myself, 1, 0)
        offset = jnp.where(stays == 1, stayed, -2 * blocks * MOVERS * cells).astype(jnp.float32)
        chosen = slot == own_start + offset
        for part, source in enumerate(sources):
            for dim in range(dims):
                comp = part * dims + dim
                row = source[dim, pl.ds(block, 1), :]
                settled[comp] = jnp.where(chosen, row, settled[comp])
        stayed += stays

    for dim in range(dims):
        halfway = settled[2 * dims + dim] + 0.5 * timestep * settled[3 * dims + dim]
        half_ref[dim] = halfway
        flat_ref[pl.ds(dim * blocks, blocks), :] = settled[dim]
        flat_ref[pl.ds((dims + dim) * blocks, blocks), :] = settled[dims + dim] + timestep * halfway
    comps = 2 * dims
    blocks_rows = []
    for block in range(blocks):
        rows = flat_ref[pl.ds(block, comps, stride=blocks), :]
        ext_ref[block] = jnp.zeros((SUBLANES, particles), jnp.float32)
        ext_ref[block, pl.ds(0, comps), :] = rows
        blocks_rows.append(rows)
    for cell in range(cells):
        for request in range(REQUESTS):
            ask = jnp.broadcast_to(ask_ref[request, pl.ds(cell, 1), :], (comps, particles))
            picked = blocks_rows[0]
            for block in range(1, blocks):
                picked = jnp.where(ask == block, blocks_rows[block], picked)
            pack_ref[cell, request] = picked

    for steps in steps_all:
        send_halo(steps, lambda cell: pack_ref.at[cell], ghosts_ref, 2)
    stores[1].start()
    taken = []
    for ghost in range(ghosts):
        device = lax.div(ghost_ref[ghost], blocks)
        rest = lax.div(device, sizes[2])
        spots = (lax.div(rest, sizes[1]), lax.rem(rest, sizes[1]), lax.rem(device, sizes[2]))
        moves = []
        for spot, place, size in zip(spots, places, sizes):
            apart = lax.rem(spot - place + size, size)
            moves.append(jnp.where(apart == size - 1, -1, apart) if size > 2 else apart)
        repeats = jnp.int32(0)
        for _, before in taken:
            repeats += jnp.where(before == device, 1, 0)
        taken.append((cell_of(places, moves, sizes) * REQUESTS + repeats, device))
    for ghost in range(ghosts):
        ext_ref[blocks + ghost] = jnp.zeros((SUBLANES, particles), jnp.float32)
    all_bytes(ghosts_ref, recv_sems.at[2], cells - 1).wait()
    for ghost, (index, _) in enumerate(taken):
        rows = ghosts_ref[lax.div(index, REQUESTS), lax.rem(index, REQUESTS)]
        ext_ref[blocks + ghost, pl.ds(0, comps), :] = rows
    stores[2].start()
    all_bytes(card_ref, send_sems.at[0], cells - 1).wait()
    all_bytes(arrived_ref, send_sems.at[1], cells - 1).wait()
    all_bytes(ghosts_ref, send_sems.at[2], cells - 1).wait()
    if far:
        all_bytes(peak_ref, send_sems.at[3], far).wait()
    for store in stores:
        store.wait()


def exchange(sizes, new_owner, ghost_ids, ref_pos, displace, velocity, acceleration):
    dims, blocks, particles = ref_pos.shape
    cells = len(neighbour_steps(sizes)) + 1
    total = sizes[0] * sizes[1] * sizes[2]
    padded = -(-cells // SUBLANES) * SUBLANES
    ghosts = ghost_ids.shape[0]
    hbm = pl.BlockSpec(memory_space=pltpu.HBM)
    outs = (
        jax.ShapeDtypeStruct((blocks + ghosts, SUBLANES, particles), jnp.float32),
        jax.ShapeDtypeStruct((dims, blocks, particles), jnp.float32),
        jax.ShapeDtypeStruct((blocks, particles), jnp.float32),
    )
    return pl.pallas_call(
        functools.partial(exchange_kernel, sizes),
        out_shape=outs,
        in_specs=[hbm] * 6,
        out_specs=(hbm, hbm, hbm),
        scratch_shapes=[
            pltpu.SMEM(new_owner.shape, jnp.int32),
            pltpu.SMEM(ghost_ids.shape, jnp.int32),
            pltpu.VMEM(ref_pos.shape, jnp.float32),
            pltpu.VMEM(ref_pos.shape, jnp.float32),
            pltpu.VMEM(ref_pos.shape, jnp.float32),
            pltpu.VMEM(ref_pos.shape, jnp.float32),
            pltpu.VMEM((cells, MOVERS * STATE, particles), jnp.float32),
            pltpu.VMEM((cells, CARD, particles), jnp.float32),
            pltpu.VMEM((total, 1, particles), jnp.float32),
            pltpu.VMEM((cells, REQUESTS, 2 * dims, particles), jnp.float32),
            pltpu.VMEM((cells, REQUESTS, 2 * dims, particles), jnp.float32),
            pltpu.VMEM((padded, particles), jnp.float32),
            pltpu.VMEM((REQUESTS, padded, particles), jnp.float32),
            pltpu.VMEM((2 * dims * blocks, particles), jnp.float32),
            *[pltpu.VMEM(out.shape, jnp.float32) for out in outs],
            pltpu.SemaphoreType.DMA((4,)),
            pltpu.SemaphoreType.DMA((4,)),
            pltpu.SemaphoreType.DMA((6,)),
            pltpu.SemaphoreType.DMA((3,)),
        ],
        compiler_params=pltpu.CompilerParams(
            collective_id=0, has_side_effects=True, vmem_limit_bytes=64 * 1024 * 1024
        ),
    )(new_owner, ghost_ids, ref_pos, displace, velocity, acceleration)


def spread_away(ready, ext_ref, rows_ref, turned_ref, sorted_ref, mask_ref, ones_ref, wide_ref):
    extended, comps, particles = ext_ref.shape
    used = wide_ref.shape[1]
    groups = wide_ref.shape[2]
    halves = sorted_ref.shape[0]
    stride = 4 * comps
    batch = particles // stride
    aligned = SUBLANES * WORD_BITS
    rows_ref[...] = jnp.zeros_like(rows_ref)
    lane = lax.broadcasted_iota(jnp.int32, mask_ref.shape[2:], 1) % particles
    for block in range(batch):
        for comp in range(used):
            keep = jnp.logical_and(lane // stride == block, lane % comps == comp)
            mask_ref[block, comp] = jnp.where(keep, 1.0, 0.0).astype(jnp.bfloat16)
    above = lax.broadcasted_iota(jnp.int32, ones_ref.shape, 0) // particles
    beside = lax.broadcasted_iota(jnp.int32, ones_ref.shape, 1) // particles
    ones_ref[...] = jnp.where(above == beside, 1.0, 0.0).astype(jnp.bfloat16)
    ready()
    for block in range(extended):
        rest = ext_ref[block]
        for term in range(3):
            part = rest.astype(jnp.bfloat16).astype(jnp.float32)
            rows_ref[pl.ds(block * stride + term * comps, comps), :] = part
            rest = rest - part
    for number in range(2 * halves):
        turned_ref[number] = rows_ref[pl.ds(number * particles, particles), :].T
    for number in range(2 * halves):
        half, column = number % halves, number // halves * particles
        for pair in range(groups // 2):
            parts = []
            for step in (2 * pair, 2 * pair + 1):
                if step < WORD_BITS:
                    parts.append(turned_ref[number, pl.ds(step, SUBLANES, stride=WORD_BITS), :])
                else:
                    start = aligned + (step - WORD_BITS) * SUBLANES
                    parts.append(turned_ref[number, pl.ds(start, SUBLANES), :])
            both = jnp.concatenate(parts, axis=0).astype(jnp.bfloat16)
            sorted_ref[half, pair, :, pl.ds(column, particles)] = both
    def spread_half(half, carry):
        table = sorted_ref[half]
        for block in range(batch):
            kept = [
                (table * mask_ref[block, comp][None]).reshape(particles, 2 * particles)
                for comp in range(used)
            ]
            spread = jnp.dot(
                jnp.concatenate(kept, axis=0), ones_ref[...], preferred_element_type=jnp.float32
            )
            for side in range(2):
                part = spread[:, side * particles : (side + 1) * particles]
                place = (half + side * halves) * batch + block
                wide_ref[place] = part.reshape(used, groups, SUBLANES, particles)
        return carry

    lax.fori_loop(0, halves, spread_half, 0)


def tail_steps(particles):
    starts = range(SUBLANES * WORD_BITS, particles, SUBLANES)
    return [(start, start // WORD_BITS, (start + SUBLANES - 1) // WORD_BITS) for start in starts]


def tile_sum(home, away, front, back, wide_ref, bit_ref, particles):
    sublane = lax.broadcasted_iota(jnp.int32, (SUBLANES, particles), 0)
    sums = [jnp.zeros((SUBLANES, particles), jnp.float32) for _ in range(3)]
    tails = tail_steps(particles)
    for step in range(particles // SUBLANES):
        if step < WORD_BITS:
            hit = jnp.bitwise_and(front, 1 << step)
        else:
            start, low, high = tails[step - WORD_BITS]
            low, high = low - SUBLANES, high - SUBLANES
            row = jnp.broadcast_to(back[low : low + 1], (SUBLANES, particles))
            if high != low:
                upper = jnp.broadcast_to(back[high : high + 1], (SUBLANES, particles))
                row = jnp.where(sublane < (high + SUBLANES) * WORD_BITS - start, row, upper)
            hit = jnp.bitwise_and(row, bit_ref[step - WORD_BITS])
        other = [wide_ref[away, comp, step] for comp in range(6)]
        ref_gap = [other[k] - home[k] for k in range(3)]
        now_gap = [ref_gap[k] + (other[3 + k] - home[3 + k]) for k in range(3)]
        ref_sq = ref_gap[0] * ref_gap[0] + ref_gap[1] * ref_gap[1] + ref_gap[2] * ref_gap[2]
        now_sq = now_gap[0] * now_gap[0] + now_gap[1] * now_gap[1] + now_gap[2] * now_gap[2]
        scaled = jnp.where(hit != 0, lax.rsqrt(ref_sq) - lax.rsqrt(now_sq), 0.0)
        sums = [sums[k] + scaled * now_gap[k] for k in range(3)]
    return sums


def bond_kernel(
    words, pairs_in, bits_in, ext_in, half_in, step_in, count_ref,
    displace_ref, velocity_ref, accel_ref,
    pairs_ref, bits_ref, ext_ref, half_ref, step_ref, rows_ref, turned_ref, sorted_ref, mask_ref, ones_ref, wide_ref,
    total_ref, bit_ref, load_sems,
):
    _, blocks, particles = accel_ref.shape
    pairs = bits_ref.shape[0] // words
    outer = (ext_in, pairs_in, bits_in, half_in, step_in)
    inner = (ext_ref, pairs_ref, bits_ref, half_ref, step_ref)
    loads = [
        pltpu.make_async_copy(source, target, load_sems.at[number])
        for number, (source, target) in enumerate(zip(outer, inner))
    ]
    for load in loads:
        load.start()
    total_ref[...] = jnp.zeros_like(total_ref)
    sublane = lax.broadcasted_iota(jnp.int32, (SUBLANES, particles), 0)
    for number, (start, _, _) in enumerate(tail_steps(particles)):
        bit_ref[number] = jnp.left_shift(1, (sublane + start) % WORD_BITS)

    spread_away(
        loads[0].wait, ext_ref, rows_ref, turned_ref, sorted_ref, mask_ref, ones_ref, wide_ref
    )

    def not_own(first, rows):
        word = lax.broadcasted_iota(jnp.int32, (rows, particles), 0) + first
        lane = lax.broadcasted_iota(jnp.int32, (rows, particles), 1)
        own = jnp.where(lane // WORD_BITS == word, jnp.left_shift(1, lane % WORD_BITS), 0)
        return jnp.bitwise_not(own)

    behind = words - SUBLANES
    keep_front, keep_back = not_own(0, SUBLANES), not_own(SUBLANES, behind)
    count = count_ref[0]
    for load in loads[1:]:
        load.wait()

    def pair_sums(wish):
        slot = jnp.minimum(wish, pairs - 1)
        live = jnp.where(wish < count, -1, 0)
        home_id = pairs_ref[0, slot]
        away_id = pairs_ref[1, slot]
        home = [
            jnp.broadcast_to(ext_ref[home_id, pl.ds(comp, 1), :], (SUBLANES, particles))
            for comp in range(6)
        ]
        apart = jnp.where(home_id == away_id, 0, -1)
        front = bits_ref[pl.ds(slot, SUBLANES, stride=pairs), :]
        back = bits_ref[pl.ds(slot + SUBLANES * pairs, behind, stride=pairs), :]
        front = front & ((keep_front | apart) & live)
        back = back & ((keep_back | apart) & live)
        return home_id, tile_sum(home, away_id, front, back, wide_ref, bit_ref, particles)

    def add_pairs(number, carry):
        found = [pair_sums(number * TOGETHER + order) for order in range(TOGETHER)]
        for home_id, sums in found:
            for comp in range(3):
                total_ref[home_id, comp] += sums[comp]
        return carry

    lax.fori_loop(0, (count + TOGETHER - 1) // TOGETHER, add_pairs, 0)
    accel = stiffness * jnp.sum(total_ref[...], axis=2)
    for comp in range(3):
        for block in range(blocks):
            accel_ref[comp, pl.ds(block, 1), :] = accel[block, comp : comp + 1]
            displace_ref[comp, pl.ds(block, 1), :] = ext_ref[block, pl.ds(3 + comp, 1), :]
        velocity_ref[comp] = half_ref[comp] + 0.5 * step_ref[...] * accel_ref[comp]


def bond_step(ext, half, step, pair_blocks, pair_count, bond_bits):
    blocks, particles = step.shape
    extended = ext.shape[0]
    words, pairs = bond_bits.shape[0:2]
    shape = jax.ShapeDtypeStruct((3, blocks, particles), jnp.float32)
    smem = pl.BlockSpec(memory_space=pltpu.SMEM)
    vmem = pl.BlockSpec(memory_space=pltpu.VMEM)
    hbm = pl.BlockSpec(memory_space=pltpu.HBM)
    groups = particles // SUBLANES
    batch = particles // (4 * SUBLANES)
    halves = -(-extended // (2 * batch))
    return pl.pallas_call(
        functools.partial(bond_kernel, words),
        out_shape=(shape, shape, shape),
        in_specs=[hbm, hbm, hbm, hbm, hbm, smem],
        out_specs=(vmem, vmem, vmem),
        scratch_shapes=[
            pltpu.SMEM(pair_blocks.shape, jnp.int32),
            pltpu.VMEM((words * pairs, particles), jnp.int32),
            pltpu.VMEM(ext.shape, jnp.float32),
            pltpu.VMEM(half.shape, jnp.float32),
            pltpu.VMEM(step.shape, jnp.float32),
            pltpu.VMEM((2 * halves * particles, particles), jnp.float32),
            pltpu.VMEM((2 * halves, particles, particles), jnp.float32),
            pltpu.VMEM((halves, groups // 2, 2 * SUBLANES, 2 * particles), jnp.bfloat16),
            pltpu.VMEM((batch, 6, 2 * SUBLANES, 2 * particles), jnp.bfloat16),
            pltpu.VMEM((2 * particles, 2 * particles), jnp.bfloat16),
            pltpu.VMEM((2 * halves * batch, 6, groups, SUBLANES, particles), jnp.float32),
            pltpu.VMEM((blocks, 3, SUBLANES, particles), jnp.float32),
            pltpu.VMEM((len(tail_steps(particles)), SUBLANES, particles), jnp.int32),
            pltpu.SemaphoreType.DMA((5,)),
        ],
        compiler_params=pltpu.CompilerParams(vmem_limit_bytes=64 * 1024 * 1024),
    )(pair_blocks, bond_bits.reshape(words * pairs, particles), ext, half, step, pair_count)


def per_device(
    ref_pos,
    displace,
    velocity,
    acceleration,
    new_owner,
    ghost_ids,
    pair_blocks,
    pair_count,
    bond_bits,
):
    sizes = tuple(lax.axis_size(name) for name in AXES)
    turned = [array.transpose(1, 0, 2) for array in (ref_pos, displace, velocity, acceleration)]
    ext, half, step = exchange(sizes, new_owner, ghost_ids, *turned)
    results = bond_step(ext, half, step, pair_blocks, pair_count, bond_bits.transpose(1, 0, 2))
    return tuple(array.transpose(1, 0, 2) for array in results)


def solution(mesh):
    in_specs = (
        P(("gx", "gy", "gz"), None, None),
        P(("gx", "gy", "gz"), None, None),
        P(("gx", "gy", "gz"), None, None),
        P(("gx", "gy", "gz"), None, None),
        P(("gx", "gy", "gz")),
        P(("gx", "gy", "gz")),
        P(None, ("gx", "gy", "gz")),
        P(("gx", "gy", "gz")),
        P(("gx", "gy", "gz"), None, None),
    )
    out_specs = (
        P(("gx", "gy", "gz"), None, None),
        P(("gx", "gy", "gz"), None, None),
        P(("gx", "gy", "gz"), None, None),
    )
    return jax.shard_map(
        per_device, mesh=mesh, in_specs=in_specs, out_specs=out_specs, check_vma=False
    )
```
